256 devices in a mesh: row: 2 (over core), col: 8 (over z), depth: 16 (over y, x).
Axes of the slice: x: 4, y: 4, z: 8, core: 2. Of those that a mesh axis runs over, the one named last changes fastest.
Arguments:
- amplitudes: bfloat16 [128, 256], P(('row', 'col'), 'depth'), may hold values from -6 to 6
- integrals: bfloat16 [1200, 307200], P('col', ('row', 'depth')), may hold values from -1 to 1
- virt_irrep: int32 [1200], replicated, may hold values from 0 to 7
- pair_irrep: int32 [128], replicated, may hold values from 0 to 7
- panel_c: int32 [256], P('depth'), may hold values from 0 to 1199
- panel_d: int32 [256], P('depth'), may hold values from 0 to 1199
Outputs:
- ladder: float32 [1200, 153600], P('col', ('row', 'depth'))
The draws below stay inside these ranges and needn't reach their ends.
All inputs are finite; a program needn't handle non-finite values.
Results may differ from the reference program's by a relative error of at most 0.0003.
Values may be sent and summed in bfloat16 or wider, within the bound.
No kernel may reach another device: no remote copies, remote signals or barrier semaphores. Data moves between devices by JAX's collectives and lax.ppermute only.
A program may use at most 192 MiB of HBM per device.

```python
import math
import jax
import jax.numpy as jnp
import numpy as np

NV = 1200
CD = 256
IRREPS = 8
IJ = 128
N_ROW = 2


def set_ends(array, stream_key, low, largest):
    dims = array.shape
    index_at = [jax.random.randint(jax.random.fold_in(stream_key, axis), (), 0, dims[axis]) for axis in range(len(dims))]
    array = array.at[tuple(index_at)].set(low)
    longest = dims.index(max(dims))
    index_at[longest] = (index_at[longest] + 1) % dims[longest]
    return array.at[tuple(index_at)].set(largest)


def shard_levels(stream_key, extent, shards, least, top_value):
    def one(dim, shards_of):
        draws = jax.random.uniform(jax.random.fold_in(jax.random.fold_in(stream_key, 6), dim), (shards_of,), jnp.float32, least / len(shards), top_value / len(shards))
        return jnp.repeat(jnp.exp(draws), extent[dim] // shards_of).reshape((-1,) + (1,) * (len(extent) - dim - 1))

    loudness = one(*shards[0])
    for cut in shards[1:]:
        loudness = loudness * one(*cut)
    return loudness


def rank_table(count, lean):
    weights = [(1 << 20) // math.isqrt(grade ** lean) + 1 for grade in range(1, count + 1)]
    scale = 1 + sum(weights) // (1 << 30)
    return np.cumsum(np.array([max(1, weight // scale) for weight in weights]))


def ranked(stream_key, extent, count, slope):
    listing = rank_table(count, slope)
    lot = jax.random.randint(jax.random.fold_in(stream_key, 1), extent, 0, int(listing[count - 1]))
    grade = jnp.searchsorted(jnp.asarray(listing, jnp.int32), lot, side="right")
    return jax.random.permutation(jax.random.fold_in(stream_key, 2), count)[grade].astype(jnp.int32)


def centred(own_key, dims, spread, reach, shards=(), kind=jnp.bfloat16):
    drawn = spread * jax.random.normal(own_key, dims, jnp.float32)
    if shards:
        drawn = drawn * shard_levels(own_key, dims, shards, -0.22, 0.18)
    return jnp.clip(drawn, -reach, reach).astype(kind)


def setup_inputs(seed: int = 0) -> dict:
    streams_of = jax.random.split(jax.random.key(seed), 7)
    amplitudes = centred(streams_of[0], (IJ, CD), 1.0, 6.0, ((0, 16), (1, 16)))
    integrals = centred(streams_of[1], (NV, CD * NV), (CD // 8) ** -0.5, 1.0, ((0, 8), (1, 32)))
    virt_irrep = set_ends(ranked(streams_of[2], (NV,), IRREPS, 1), jax.random.fold_in(streams_of[2], 3), 0, IRREPS - 1).astype(jnp.int32)
    pair_irrep = set_ends(jax.random.randint(streams_of[3], (IJ,), 0, IRREPS), jax.random.fold_in(streams_of[3], 1), 0, IRREPS - 1).astype(jnp.int32)
    panel_c = set_ends(jax.random.randint(streams_of[4], (CD,), 0, NV), jax.random.fold_in(streams_of[4], 1), 0, NV - 1).astype(jnp.int32)
    panel_d = set_ends(jax.random.randint(streams_of[5], (CD,), 0, NV), jax.random.fold_in(streams_of[5], 1), 0, NV - 1).astype(jnp.int32)
    return {"amplitudes": amplitudes, "integrals": integrals, "virt_irrep": virt_irrep, "pair_irrep": pair_irrep, "panel_c": panel_c, "panel_d": panel_d}


def reference(amplitudes, integrals, virt_irrep, pair_irrep, panel_c, panel_d):
    block_a = NV // N_ROW
    pair_sym = jnp.bitwise_xor(virt_irrep[panel_c], virt_irrep[panel_d])
    keep = pair_irrep[:, None] == pair_sym[None, :]
    allowed = jnp.where(keep, amplitudes, jnp.zeros_like(amplitudes)).astype(jnp.bfloat16)
    panels = integrals.reshape(NV, N_ROW, CD, block_a).astype(jnp.float32)
    full = jnp.einsum("jc,brca->brja", allowed.astype(jnp.float32), panels)
    irrep_a = virt_irrep.reshape(N_ROW, block_a)
    ab_sym = jnp.bitwise_xor(virt_irrep[:, None, None, None], irrep_a[None, :, None, :])
    mask = pair_irrep[None, None, :, None] == ab_sym
    ladder = jnp.where(mask, full, jnp.float32(0.0))
    return ladder.reshape(NV, N_ROW * IJ * block_a)
```

```python
import jax
import jax.numpy as jnp
from jax import lax
from jax.experimental import pallas as pl
from jax.experimental.pallas import tpu as pltpu
from jax.sharding import PartitionSpec as P

NV = 1200
LAYERS = 16
A_ROWS = 600
B_COLS = 150
A_PAD = 640
B_PAD = 160
CDS = 16
OWN_IJ = 8
CAP_IN = 40
CAP_OUT = 24
PER = 10
META = A_ROWS - 512
BF = jnp.bfloat16
F32 = jnp.float32
I32 = jnp.int32
VMEM_LIMIT = 48 * 1024 * 1024
DN = (((1,), (0,)), ((), ()))


def iota(shape, dim):
    return lax.broadcasted_iota(I32, shape, dim)


def dot(x, y):
    return lax.dot_general(x, y, DN, preferred_element_type=F32)


def to_col(row):
    size = row.shape[1]
    eye = iota((size, size), 0) == iota((size, size), 1)
    spread = jnp.where(eye, jnp.broadcast_to(row.astype(F32), (size, size)), 0.0)
    return jnp.sum(spread, axis=1, keepdims=True).astype(I32)


def ones(mask):
    return jnp.where(mask, 1.0, 0.0)


def ranks(b_row):
    key_row = b_row * 256 + iota(b_row.shape, 1)
    key_col = to_col(key_row)
    rank_row = jnp.sum(ones(key_col < key_row), axis=0, keepdims=True).astype(I32)
    rank_col = jnp.sum(ones(key_row < key_col), axis=1, keepdims=True).astype(I32)
    return rank_row, rank_col, jnp.right_shift(key_col, 8)


def class_counts(labels):
    count = [sum((label == y).astype(I32) for label in labels) for y in range(8)]
    order = [sum([(labels[k] == labels[j]).astype(I32) for k in range(j)], jnp.int32(0)) for j in range(len(labels))]
    return count, order


def pack_kernel(virt, panel_c, panel_d, pair, b_ref, a_ref, amp_ref, eri_ref, x_ref, hot, masked, q_ref, s_ref, m_ref, meta):
    me = lax.axis_index("depth")
    g = [virt[panel_c[j]] ^ virt[panel_d[j]] for j in range(CDS)]
    b_row = b_ref[...]
    rank_row, rank_col, b_col = ranks(b_row)
    same = jnp.logical_and((rank_row & 15) == (rank_col & 15), rank_col < rank_row)
    diff = b_col ^ b_row
    before = [jnp.sum(ones(jnp.logical_and(same, diff == y)), axis=0, keepdims=True) for y in range(8)]

    def places(labels):
        count, order = class_counts(labels)
        count = [c.astype(F32) for c in count]
        for x in range(8):
            s_ref[x : x + 1, :] = sum(count[y ^ x] * before[y] for y in range(8))
        return [s_ref[pl.ds(labels[j], 1), :] + order[j].astype(F32) for j in range(len(labels))]

    real = iota((1, B_PAD), 1) < B_COLS
    out_places = places([pair[me * OWN_IJ + j] for j in range(OWN_IJ)])
    top_out = jnp.max(jnp.where(real, sum_max(out_places), 0.0), axis=1, keepdims=True)
    in_places = places(g)
    top_in = jnp.max(jnp.where(real, sum_max(in_places), 0.0), axis=1, keepdims=True)
    over = jnp.maximum(ones(top_out >= CAP_OUT), ones(top_in >= CAP_IN))
    first = (rank_row & 15) * CAP_IN
    for j in range(CDS):
        q_ref[0:1, j * B_PAD : (j + 1) * B_PAD] = first + in_places[j].astype(I32)
    rows = LAYERS * CAP_IN
    for t in range(CDS * B_PAD // 512):
        at = slice(t * 512, (t + 1) * 512)
        hot[:, at] = ones(iota((rows, 512), 0) == q_ref[0:1, at]).astype(BF)

    masked[...] = jnp.zeros_like(masked)
    ab = (b_col ^ a_ref[...])[:B_COLS, :A_ROWS].astype(F32).astype(BF)
    for j in range(CDS):
        slab = eri_ref[:, j * A_ROWS : (j + 1) * A_ROWS]
        label = jnp.full((1, 1), g[j].astype(F32), F32).astype(BF)
        masked[j * B_PAD : j * B_PAD + B_COLS, 0:A_ROWS] = jnp.where(ab == label, slab, jnp.zeros_like(slab))

    m_ref[...] = jnp.zeros_like(m_ref)
    m_ref[0:8, META : META + CDS] = amp_ref[...].astype(F32)
    lane = iota((1, CDS), 1)
    m_ref[8:9, META : META + CDS] = sum(jnp.where(lane == j, g[j], 0) for j in range(CDS)).astype(F32)
    m_ref[9:10, META : META + CDS] = jnp.broadcast_to(over, (1, CDS))
    meta[...] = jnp.zeros_like(meta)
    for e in range(LAYERS):
        meta[e * CAP_IN : e * CAP_IN + 16, :] = m_ref[...]
    for n in (0, 256):
        x_ref[:, n : n + 256] = dot(hot[...], masked[:, n : n + 256]).astype(BF)
    x_ref[:, 512:640] = (dot(hot[...], masked[:, 512:640]) + meta[...]).astype(BF)


def sum_max(terms):
    top = terms[0]
    for term in terms[1:]:
        top = jnp.maximum(top, term)
    return top


def compute_kernel(b_ref, a_ref, pair_ref, r_ref, y_ref, x_ref, hot, eri, amp, hot2, amps):
    me = lax.axis_index("depth")
    b_row = b_ref[...]
    rank_row, _, _ = ranks(b_row)
    beta = []
    for i in range(PER):
        mine = rank_row == i * LAYERS + me
        beta.append(jnp.sum(jnp.where(mine, b_row, 0).astype(F32), axis=1, keepdims=True).astype(I32))

    g_row = r_ref[0, 8:9, :].astype(F32).astype(I32)
    g_col = to_col(g_row)
    wide = (256, 256)
    same = jnp.right_shift(iota(wide, 0), 4) == jnp.right_shift(iota(wide, 1), 4)
    earlier = jnp.logical_and(same, iota(wide, 1) < iota(wide, 0))
    order = jnp.sum(ones(jnp.logical_and(earlier, g_row == g_col)), axis=1, keepdims=True)
    lane = iota((1, 128), 1)
    part, label = jnp.right_shift(lane, 3), lane & 7
    own = sum(jnp.where(part == i, beta[i], 0) for i in range(PER))
    wanted = (label ^ own) ^ g_col
    seen = sum(ones(jnp.logical_and(part > i, wanted == beta[i])) for i in range(PER - 1))
    count = dot(ones(same).astype(BF), ones(g_col == label).astype(BF))
    square = (128, 128)
    by_part = ones(jnp.right_shift(iota(square, 0), 3) == iota(square, 1)).astype(BF)
    place = dot((seen * count).astype(BF), by_part) + order
    rows = iota((256, 1), 0)
    place = place.astype(I32) + (jnp.right_shift(rows, 4) & 3) * CAP_IN

    four = 4 * CAP_IN
    sym = [a_ref[...] ^ beta[i] for i in range(PER)]
    for k in range(4):
        at = slice(k * 64, (k + 1) * 64)
        for i in range(PER):
            hot[i * 64 : (i + 1) * 64, :] = ones(iota((64, four), 1) == place[at, i : i + 1]).astype(BF)
        for n, w in ((0, 256), (256, 256), (512, 128)):
            got = dot(hot[...], y_ref[k * four : (k + 1) * four, n : n + w])
            for i in range(PER):
                keep = sym[i][:, n : n + w] == g_col[at, :]
                eri[i * 256 + k * 64 : i * 256 + (k + 1) * 64, n : n + w] = jnp.where(
                    keep, got[i * 64 : (i + 1) * 64, :], 0.0
                ).astype(BF)

    p_row = pair_ref[...]
    p_col = to_col(p_row)
    for c in range(LAYERS):
        amps[c * 8 : (c + 1) * 8, :] = r_ref[c, 0:8, :].astype(F32)
    allowed = jnp.where(p_col == g_row, amps[...], 0.0).astype(BF)
    same2 = jnp.right_shift(iota(square, 0), 3) == jnp.right_shift(iota(square, 1), 3)
    earlier2 = jnp.logical_and(same2, iota(square, 0) < iota(square, 1))
    order2 = jnp.sum(ones(jnp.logical_and(earlier2, p_row == p_col)), axis=0, keepdims=True)
    row = iota((128, 1), 0)
    part2, label2 = jnp.right_shift(row, 3), row & 7
    own2 = sum(jnp.where(part2 == i, beta[i], 0) for i in range(PER))
    wanted2 = (label2 ^ own2) ^ p_row
    seen2 = sum(ones(jnp.logical_and(part2 > i, wanted2 == beta[i])) for i in range(PER - 1))
    count2 = dot(ones(label2 == p_row).astype(BF), ones(same2).astype(BF))
    short = (16, 128)
    by_part2 = ones(jnp.right_shift(iota(short, 1), 3) == iota(short, 0)).astype(BF)
    place2 = dot(by_part2, (seen2 * count2).astype(BF)) + order2
    place2 = place2.astype(I32) + jnp.right_shift(iota((1, 128), 1), 3) * CAP_OUT
    out_rows = LAYERS * CAP_OUT
    for i in range(PER):
        hot2[...] = ones(iota((out_rows, 128), 0) == place2[i : i + 1, :]).astype(BF)
        amp[:, i * 256 : (i + 1) * 256] = dot(hot2[...], allowed).astype(BF)
    for n, w in ((0, 256), (256, 256), (512, 128)):
        x_ref[:, n : n + w] = dot(amp[...], eri[:, n : n + w])


def unpack_kernel(pair, b_ref, a_ref, y_ref, o_ref, hot, high, low, j_ref):
    me = lax.axis_index("depth")
    labels = [pair[me * OWN_IJ + j] for j in range(OWN_IJ)]
    count, order = class_counts(labels)
    for y in range(8):
        j_ref[y] = count[y]
    b_row = b_ref[...]
    rank_row, rank_col, b_col = ranks(b_row)
    same = jnp.logical_and((rank_row & 15) == (rank_col & 15), rank_row < rank_col)
    diff = b_col ^ b_row
    before = [jnp.sum(ones(jnp.logical_and(same, diff == y)), axis=1, keepdims=True) for y in range(8)]
    first = (rank_col & 15) * CAP_OUT
    width = LAYERS * CAP_OUT
    for j in range(OWN_IJ):
        place = sum(j_ref[y ^ labels[j]].astype(F32) * before[y] for y in range(8)) + order[j].astype(F32)
        hot[j * B_PAD : (j + 1) * B_PAD, :] = ones(iota((B_PAD, width), 1) == first + place.astype(I32)).astype(BF)
    whole = y_ref[...]
    top = whole.astype(BF)
    high[...] = top
    low[...] = (whole - top.astype(F32)).astype(BF)
    ab = b_col ^ a_ref[...]
    for j in range(OWN_IJ):
        got = dot(hot[j * B_PAD : (j + 1) * B_PAD, :], high[...]) + dot(hot[j * B_PAD : (j + 1) * B_PAD, :], low[...])
        got = jnp.where(ab == labels[j], got, 0.0)
        o_ref[:, j * A_ROWS : (j + 1) * A_ROWS] = got[:B_COLS, :A_ROWS]


VM = pl.BlockSpec(memory_space=pltpu.VMEM)
SM = pl.BlockSpec(memory_space=pltpu.SMEM)


def call(kernel, args, specs, out, scratch, flops, moved):
    return pl.pallas_call(
        kernel,
        out_shape=out,
        in_specs=specs,
        out_specs=VM,
        scratch_shapes=scratch,
        compiler_params=pltpu.CompilerParams(vmem_limit_bytes=VMEM_LIMIT),
        cost_estimate=pl.CostEstimate(flops=flops, bytes_accessed=moved, transcendentals=0),
    )(*args)


def dense(amplitudes, integrals, virt_irrep, pair_irrep, panel_c, panel_d):
    gathered = lax.all_gather(amplitudes, ("row", "col"), axis=0, tiled=True)
    pair_sym = jnp.bitwise_xor(virt_irrep[panel_c], virt_irrep[panel_d])
    keep = pair_irrep[:, None] == pair_sym[None, :]
    allowed = jnp.where(keep, gathered, jnp.zeros_like(gathered))
    own_rows = allowed.shape[0] // LAYERS
    mine = lax.all_to_all(allowed, "depth", split_axis=0, concat_axis=1, tiled=True)
    piece = lax.all_gather(integrals, "depth", axis=1, tiled=True)
    shaped = piece.reshape(B_COLS, piece.shape[1] // A_ROWS, A_ROWS)
    full = jnp.einsum("jc,bca->jba", mine, shaped, preferred_element_type=F32)
    irrep_a = lax.dynamic_slice_in_dim(virt_irrep, lax.axis_index("row") * A_ROWS, A_ROWS, 0)
    irrep_b = lax.dynamic_slice_in_dim(virt_irrep, lax.axis_index("col") * B_COLS, B_COLS, 0)
    irrep_ij = lax.dynamic_slice_in_dim(pair_irrep, lax.axis_index("depth") * own_rows, own_rows, 0)
    ab_sym = jnp.bitwise_xor(irrep_b[:, None], irrep_a[None, :])
    mask = irrep_ij[:, None, None] == ab_sym[None, :, :]
    masked = jnp.where(mask, full, jnp.float32(0.0))
    return jnp.transpose(masked, (1, 0, 2)).reshape(B_COLS, own_rows * A_ROWS)


def body(amplitudes, integrals, virt_irrep, pair_irrep, panel_c, panel_d):
    irrep_a = lax.dynamic_slice_in_dim(virt_irrep, lax.axis_index("row") * A_ROWS, A_ROWS, 0)
    irrep_b = lax.dynamic_slice_in_dim(virt_irrep, lax.axis_index("col") * B_COLS, B_COLS, 0)
    a_row = jnp.pad(irrep_a, (0, A_PAD - A_ROWS), constant_values=64)[None, :]
    b_row = jnp.pad(irrep_b, (0, B_PAD - B_COLS), constant_values=16)[None, :]
    rows = LAYERS * CAP_IN
    sent = call(
        pack_kernel,
        (virt_irrep, panel_c, panel_d, pair_irrep, b_row, a_row, amplitudes, integrals),
        [SM, SM, SM, SM, VM, VM, VM, VM],
        jax.ShapeDtypeStruct((rows, A_PAD), BF),
        [
            pltpu.VMEM((rows, CDS * B_PAD), BF),
            pltpu.VMEM((CDS * B_PAD, A_PAD), BF),
            pltpu.VMEM((8, CDS * B_PAD), I32),
            pltpu.VMEM((8, B_PAD), F32),
            pltpu.VMEM((16, 128), F32),
            pltpu.VMEM((rows, 128), F32),
        ],
        2 * rows * CDS * B_PAD * A_PAD,
        2 * B_COLS * CDS * A_ROWS,
    )
    held = lax.all_to_all(sent.reshape(LAYERS, CAP_IN, A_PAD), "depth", 0, 0, tiled=True)
    small = held[:, 0:16, A_ROWS : A_ROWS + CDS].transpose(1, 0, 2).reshape(16, LAYERS * CDS)
    shared = lax.all_to_all(jnp.broadcast_to(small[None], (16, 16, LAYERS * CDS)), ("row", "col"), 0, 0, tiled=True)
    over = jnp.max(shared[:, 9, :].astype(F32)) > 0.5

    def packed(shared, held):
        out_rows = LAYERS * CAP_OUT
        part = call(
            compute_kernel,
            (b_row, a_row, pair_irrep[None, :], shared, held.reshape(rows, A_PAD)),
            [VM] * 5,
            jax.ShapeDtypeStruct((out_rows, A_PAD), F32),
            [
                pltpu.VMEM((PER * 64, 4 * CAP_IN), BF),
                pltpu.VMEM((PER * 256, A_PAD), BF),
                pltpu.VMEM((out_rows, PER * 256), BF),
                pltpu.VMEM((out_rows, 128), BF),
                pltpu.VMEM((128, 256), F32),
            ],
            2 * PER * 256 * A_PAD * (out_rows + 4 * CAP_IN),
            2 * rows * A_PAD,
        )
        back = lax.all_to_all(part.reshape(LAYERS, CAP_OUT, A_PAD), "depth", 0, 0, tiled=True)
        return call(
            unpack_kernel,
            (pair_irrep, b_row, a_row, back.reshape(out_rows, A_PAD)),
            [SM, VM, VM, VM],
            jax.ShapeDtypeStruct((B_COLS, OWN_IJ * A_ROWS), F32),
            [
                pltpu.VMEM((OWN_IJ * B_PAD, out_rows), BF),
                pltpu.VMEM((out_rows, A_PAD), BF),
                pltpu.VMEM((out_rows, A_PAD), BF),
                pltpu.SMEM((8,), I32),
            ],
            4 * OWN_IJ * B_PAD * out_rows * A_PAD,
            4 * B_COLS * OWN_IJ * A_ROWS,
        )

    def general(shared, held):
        return dense(amplitudes, integrals, virt_irrep, pair_irrep, panel_c, panel_d)

    return lax.cond(over, general, packed, shared, held)


def solution(mesh):
    return jax.shard_map(
        body,
        mesh=mesh,
        in_specs=(
            P(("row", "col"), "depth"),
            P("col", ("row", "depth")),
            P(),
            P(),
            P("depth"),
            P("depth"),
        ),
        out_specs=P("col", ("row", "depth")),
        check_vma=False,
    )
```

```python
import jax
import jax.numpy as jnp
from jax import lax
from jax.experimental import pallas as pl
from jax.experimental.pallas import tpu as pltpu
from jax.sharding import PartitionSpec as P

NV = 1200
LAYERS = 16
A_ROWS = 600
B_COLS = 150
A_PAD = 640
B_PAD = 160
CDS = 16
OWN_IJ = 8
CAP_IN = 40
CAP_OUT = 24
PER = 10
TURN = 1280
META = A_ROWS - 512
BF = jnp.bfloat16
F32 = jnp.float32
I32 = jnp.int32
VMEM_LIMIT = 48 * 1024 * 1024
DN = (((1,), (0,)), ((), ()))


def iota(shape, dim):
    return lax.broadcasted_iota(I32, shape, dim)


def dot(x, y):
    return lax.dot_general(x, y, DN, preferred_element_type=F32)


def to_col(row):
    size = row.shape[1]
    eye = iota((size, size), 0) == iota((size, size), 1)
    spread = jnp.where(eye, jnp.broadcast_to(row.astype(F32), (size, size)), 0.0)
    return jnp.sum(spread, axis=1, keepdims=True).astype(I32)


def ones(mask):
    return jnp.where(mask, 1.0, 0.0)


def ranks(b_row):
    key_row = b_row * 256 + iota(b_row.shape, 1)
    key_col = to_col(key_row)
    rank_row = jnp.sum(ones(key_col < key_row), axis=0, keepdims=True).astype(I32)
    rank_col = jnp.sum(ones(key_row < key_col), axis=1, keepdims=True).astype(I32)
    return rank_row, rank_col, jnp.right_shift(key_col, 8)


def irreps(v_ref, turn):
    turn[:, 0:NV] = jnp.broadcast_to(v_ref[...], (8, NV))
    turn[:, NV:] = jnp.zeros((8, TURN - NV), I32)
    whole = turn[...]
    a_at = lax.axis_index("row") * A_ROWS
    b_at = lax.axis_index("col") * B_COLS
    a_row = pltpu.roll(whole, TURN - a_at, 1)[0:1, 0:A_PAD]
    b_row = pltpu.roll(whole, TURN - b_at, 1)[0:1, 0:B_PAD]
    a_row = jnp.where(iota((1, A_PAD), 1) < A_ROWS, a_row, 64)
    return a_row, jnp.where(iota((1, B_PAD), 1) < B_COLS, b_row, 16)


def class_counts(labels):
    count = [sum((label == y).astype(I32) for label in labels) for y in range(8)]
    order = [sum([(labels[k] == labels[j]).astype(I32) for k in range(j)], jnp.int32(0)) for j in range(len(labels))]
    return count, order


def slots(pair_ref):
    p_row = pair_ref[...]
    p_col = to_col(p_row)
    square = (128, 128)
    alike = p_row == p_col
    row = jnp.sum(ones(jnp.logical_and(alike, iota(square, 0) < iota(square, 1))), axis=0, keepdims=True)
    col = jnp.sum(ones(jnp.logical_and(alike, iota(square, 1) < iota(square, 0))), axis=1, keepdims=True)
    return row.astype(I32), col.astype(I32), p_col


def place_kernel(virt, panel, pair, v_ref, pair_ref, q_ref, m_ref, s_ref, turn, each):
    me = lax.axis_index("depth")
    _, b_row = irreps(v_ref, turn)
    g = [virt[panel[j]] ^ virt[panel[CDS + j]] for j in range(CDS)]
    rank_row, rank_col, b_col = ranks(b_row)
    same = jnp.logical_and((rank_row & 15) == (rank_col & 15), rank_col < rank_row)
    diff = b_col ^ b_row
    before = [jnp.sum(ones(jnp.logical_and(same, diff == y)), axis=0, keepdims=True) for y in range(8)]
    count, order = class_counts(g)
    count = [c.astype(F32) for c in count]
    for x in range(8):
        s_ref[x : x + 1, :] = sum(count[y ^ x] * before[y] for y in range(8))
    first = (rank_row & 15) * CAP_IN
    for j in range(CDS):
        place = s_ref[pl.ds(g[j], 1), :] + order[j].astype(F32)
        q_ref[0:1, j * B_PAD : (j + 1) * B_PAD] = first + place.astype(I32)

    own = [pair[me * OWN_IJ + j] for j in range(OWN_IJ)]
    for c in range(8):
        each[c : c + 1, 0:B_COLS] = turn[0:1, c * B_COLS : (c + 1) * B_COLS]
    of_col = each[:, 0:B_COLS]
    chunk = jnp.maximum(15 - iota((8, 128), 1), 0)
    start = jnp.zeros((8, 1), I32)
    dealt = []
    for h in range(8):
        end = start + jnp.sum(ones(of_col == h), axis=1, keepdims=True).astype(I32)
        dealt.append((jnp.right_shift(end + chunk, 4) - jnp.right_shift(start + chunk, 4)).astype(F32))
        start = end
    over = jnp.zeros((8, 128), F32)
    for counts, cap in ((count, CAP_IN), ([c.astype(F32) for c in class_counts(own)[0]], CAP_OUT)):
        for x in range(8):
            stacked = sum(counts[y ^ x] * dealt[y] for y in range(8))
            over = jnp.maximum(over, ones(stacked > cap))
    slot_row, _, _ = slots(pair_ref)
    over = jnp.maximum(jnp.max(over, axis=(0, 1), keepdims=True), ones(jnp.max(slot_row, axis=1, keepdims=True) >= CAP_IN))
    lane = iota((1, CDS), 1)
    m_ref[...] = jnp.zeros_like(m_ref)
    m_ref[0:1, META + CDS : META + 2 * CDS] = sum(jnp.where(lane == j, g[j], 0) for j in range(CDS)).astype(F32)
    m_ref[1:2, META + CDS : META + 2 * CDS] = jnp.broadcast_to(over, (1, CDS))


def pack_kernel(g_ref, v_ref, q_ref, eri_ref, x_ref, hot, masked, turn):
    a_row, b_row = irreps(v_ref, turn)
    b_col = to_col(b_row)
    rows = LAYERS * CAP_IN
    for t in range(CDS * B_PAD // 512):
        at = slice(t * 512, (t + 1) * 512)
        hot[:, at] = ones(iota((rows, 512), 0) == q_ref[0:1, at]).astype(BF)
    masked[...] = jnp.zeros_like(masked)
    ab = (b_col ^ a_row)[:B_COLS, :A_ROWS].astype(F32).astype(BF)
    for j in range(CDS):
        slab = eri_ref[:, j * A_ROWS : (j + 1) * A_ROWS]
        label = g_ref[0:1, META + CDS + j : META + CDS + j + 1].astype(BF)
        masked[j * B_PAD : j * B_PAD + B_COLS, 0:A_ROWS] = jnp.where(ab == label, slab, jnp.zeros_like(slab))
    for n, w in ((0, 256), (256, 256), (512, 128)):
        x_ref[:, n : n + w] = dot(hot[...], masked[:, n : n + w]).astype(BF)


def note_kernel(g_ref, pair_ref, amp_ref, x_in, x_ref, m_ref, amps):
    slot_row, _, p_col = slots(pair_ref)
    g_row = g_ref[0:1, META + CDS : META + 2 * CDS].astype(I32)
    for k in range(16):
        block = (lax.axis_index("row") ^ (k & 1)) * 8 + (lax.axis_index("col") ^ (k >> 1))
        amps[pl.ds(pl.multiple_of(block * 8, 8), 8), :] = amp_ref[k * 8 : (k + 1) * 8, :].astype(F32)
    allowed = jnp.where(p_col == g_row, amps[...], 0.0).astype(BF)
    in_slot = ones(iota((CAP_IN, 128), 0) == slot_row).astype(BF)
    m_ref[...] = g_ref[...]
    m_ref[:, META : META + CDS] = dot(in_slot, allowed)
    note = m_ref[...]
    whole = jnp.concatenate([note] * LAYERS, axis=0)
    x_ref[...] = (x_in[...].astype(F32) + whole).astype(BF)


def compute_kernel(v_ref, pair_ref, r_ref, y_ref, x_ref, hot, eri, amp, hot2, turn):
    me = lax.axis_index("depth")
    a_row, b_row = irreps(v_ref, turn)
    rank_row, _, _ = ranks(b_row)
    beta = []
    for i in range(PER):
        mine = rank_row == i * LAYERS + me
        beta.append(jnp.sum(jnp.where(mine, b_row, 0).astype(F32), axis=1, keepdims=True).astype(I32))

    g_row = r_ref[1, 0:1, :].astype(F32).astype(I32)
    g_col = to_col(g_row)
    wide = (256, 256)
    same = jnp.right_shift(iota(wide, 0), 4) == jnp.right_shift(iota(wide, 1), 4)
    earlier = jnp.logical_and(same, iota(wide, 1) < iota(wide, 0))
    order = jnp.sum(ones(jnp.logical_and(earlier, g_row == g_col)), axis=1, keepdims=True)
    lane = iota((1, 128), 1)
    part, label = jnp.right_shift(lane, 3), lane & 7
    own = sum(jnp.where(part == i, beta[i], 0) for i in range(PER))
    wanted = (label ^ own) ^ g_col
    seen = sum(ones(jnp.logical_and(part > i, wanted == beta[i])) for i in range(PER - 1))
    count = dot(ones(same).astype(BF), ones(g_col == label).astype(BF))
    square = (128, 128)
    by_part = ones(jnp.right_shift(iota(square, 0), 3) == iota(square, 1)).astype(BF)
    place = dot((seen * count).astype(BF), by_part) + order
    rows = iota((256, 1), 0)
    place = place.astype(I32) + (jnp.right_shift(rows, 4) & 3) * CAP_IN

    four = 4 * CAP_IN
    sym = [a_row ^ beta[i] for i in range(PER)]
    for k in range(4):
        at = slice(k * 64, (k + 1) * 64)
        for i in range(PER):
            hot[i * 64 : (i + 1) * 64, :] = ones(iota((64, four), 1) == place[at, i : i + 1]).astype(BF)
        for n, w in ((0, 256), (256, 256), (512, 128)):
            got = dot(hot[...], y_ref[k * four : (k + 1) * four, n : n + w])
            for i in range(PER):
                keep = sym[i][:, n : n + w] == g_col[at, :]
                eri[i * 256 + k * 64 : i * 256 + (k + 1) * 64, n : n + w] = jnp.where(
                    keep, got[i * 64 : (i + 1) * 64, :], 0.0
                ).astype(BF)

    p_row = pair_ref[...]
    _, slot_col, p_col = slots(pair_ref)
    from_slot = ones(iota((128, CAP_IN), 1) == slot_col).astype(BF)
    allowed = jnp.where(p_col == g_row, dot(from_slot, r_ref[0]), 0.0).astype(BF)
    same2 = jnp.right_shift(iota(square, 0), 3) == jnp.right_shift(iota(square, 1), 3)
    earlier2 = jnp.logical_and(same2, iota(square, 0) < iota(square, 1))
    order2 = jnp.sum(ones(jnp.logical_and(earlier2, p_row == p_col)), axis=0, keepdims=True)
    row = iota((128, 1), 0)
    part2, label2 = jnp.right_shift(row, 3), row & 7
    own2 = sum(jnp.where(part2 == i, beta[i], 0) for i in range(PER))
    wanted2 = (label2 ^ own2) ^ p_row
    seen2 = sum(ones(jnp.logical_and(part2 > i, wanted2 == beta[i])) for i in range(PER - 1))
    count2 = dot(ones(label2 == p_row).astype(BF), ones(same2).astype(BF))
    short = (16, 128)
    by_part2 = ones(jnp.right_shift(iota(short, 1), 3) == iota(short, 0)).astype(BF)
    place2 = dot(by_part2, (seen2 * count2).astype(BF)) + order2
    place2 = place2.astype(I32) + (LAYERS - 1 - jnp.right_shift(iota((1, 128), 1), 3)) * CAP_OUT
    out_rows = LAYERS * CAP_OUT
    for i in range(PER):
        hot2[...] = ones(iota((out_rows, 128), 0) == place2[i : i + 1, :]).astype(BF)
        amp[:, i * 256 : (i + 1) * 256] = dot(hot2[...], allowed).astype(BF)
    for n, w in ((0, 256), (256, 256), (512, 128)):
        x_ref[:, n : n + w] = dot(amp[...], eri[:, n : n + w])


def unpack_kernel(pair, v_ref, y_ref, o_ref, hot, high, low, j_ref, turn):
    me = lax.axis_index("depth")
    a_row, b_row = irreps(v_ref, turn)
    labels = [pair[me * OWN_IJ + j] for j in range(OWN_IJ)]
    count, order = class_counts(labels)
    for y in range(8):
        j_ref[y] = count[y]
    rank_row, rank_col, b_col = ranks(b_row)
    same = jnp.logical_and((rank_row & 15) == (rank_col & 15), rank_row < rank_col)
    diff = b_col ^ b_row
    before = [jnp.sum(ones(jnp.logical_and(same, diff == y)), axis=1, keepdims=True) for y in range(8)]
    first = (LAYERS - 1 - (rank_col & 15)) * CAP_OUT
    width = LAYERS * CAP_OUT
    for j in range(OWN_IJ):
        place = sum(j_ref[y ^ labels[j]].astype(F32) * before[y] for y in range(8)) + order[j].astype(F32)
        hot[j * B_PAD : (j + 1) * B_PAD, :] = ones(iota((B_PAD, width), 1) == first + place.astype(I32)).astype(BF)
    whole = y_ref[...]
    top = whole.astype(BF)
    high[...] = top
    low[...] = (whole - top.astype(F32)).astype(BF)
    ab = b_col ^ a_row
    for j in range(OWN_IJ):
        got = dot(hot[j * B_PAD : (j + 1) * B_PAD, :], high[...]) + dot(hot[j * B_PAD : (j + 1) * B_PAD, :], low[...])
        got = jnp.where(ab == labels[j], got, 0.0)
        o_ref[:, j * A_ROWS : (j + 1) * A_ROWS] = got[:B_COLS, :A_ROWS]


VM = pl.BlockSpec(memory_space=pltpu.VMEM)
SM = pl.BlockSpec(memory_space=pltpu.SMEM)


def call(kernel, args, specs, out, scratch, flops, moved):
    return pl.pallas_call(
        kernel,
        out_shape=out,
        in_specs=specs,
        out_specs=[VM] * len(out) if isinstance(out, tuple) else VM,
        scratch_shapes=scratch,
        compiler_params=pltpu.CompilerParams(vmem_limit_bytes=VMEM_LIMIT),
        cost_estimate=pl.CostEstimate(flops=flops, bytes_accessed=moved, transcendentals=0),
    )(*args)


def dense(rows, shared, integrals, virt_irrep, pair_irrep):
    rows = rows.reshape(LAYERS, OWN_IJ, CDS)
    at = jnp.arange(LAYERS)
    at = (lax.axis_index("row") ^ (at >> 3)) + 2 * (lax.axis_index("col") ^ (at & 7))
    amps = jnp.take(rows, at, axis=0).reshape(1, LAYERS * OWN_IJ, CDS)
    amps = jnp.broadcast_to(amps, (LAYERS, LAYERS * OWN_IJ, CDS))
    amps = lax.all_to_all(amps, "depth", 0, 0, tiled=True).transpose(1, 0, 2).reshape(-1, LAYERS * CDS)
    pair_sym = shared[1, 0, :].astype(I32)
    allowed = jnp.where(pair_irrep[:, None] == pair_sym[None, :], amps, jnp.zeros_like(amps))
    share = B_PAD // LAYERS
    padded = jnp.pad(integrals, ((0, B_PAD - B_COLS), (0, 0))).reshape(LAYERS, share, CDS * A_ROWS)
    piece = lax.all_to_all(padded, "depth", 0, 0, tiled=True).reshape(LAYERS, share, CDS, A_ROWS)
    full = jnp.einsum("jsc,sbca->jba", allowed.reshape(-1, LAYERS, CDS), piece, preferred_element_type=F32)
    back = lax.all_to_all(full, "depth", 0, 0, tiled=True).reshape(LAYERS, OWN_IJ, share, A_ROWS)
    mine = back.transpose(0, 2, 1, 3).reshape(B_PAD, OWN_IJ, A_ROWS)[:B_COLS]
    irrep_a = lax.dynamic_slice_in_dim(virt_irrep, lax.axis_index("row") * A_ROWS, A_ROWS, 0)
    irrep_b = lax.dynamic_slice_in_dim(virt_irrep, lax.axis_index("col") * B_COLS, B_COLS, 0)
    irrep_ij = lax.dynamic_slice_in_dim(pair_irrep, lax.axis_index("depth") * OWN_IJ, OWN_IJ, 0)
    ab_sym = jnp.bitwise_xor(irrep_b[:, None], irrep_a[None, :])
    mask = irrep_ij[None, :, None] == ab_sym[:, None, :]
    return jnp.where(mask, mine, jnp.float32(0.0)).reshape(B_COLS, OWN_IJ * A_ROWS)


def swap(array, axis, size, step):
    return lax.ppermute(array, axis, [(d, d ^ step) for d in range(size)])


def body(amplitudes, integrals, virt_irrep, pair_irrep, panel_c, panel_d):
    rows = LAYERS * CAP_IN
    out_rows = LAYERS * CAP_OUT
    p_row = pair_irrep[None, :]
    turn = pltpu.VMEM((8, TURN), I32)
    amps = jnp.concatenate([amplitudes, swap(amplitudes, "row", 2, 1)], axis=0)
    amps, virt_irrep, panel_c, panel_d = lax.optimization_barrier((amps, virt_irrep, panel_c, panel_d))
    near = swap(amps, "col", 8, 1)
    v_row = virt_irrep[None, :]
    panel = jnp.concatenate([panel_c, panel_d])
    near, v_row, panel = lax.optimization_barrier((near, v_row, panel))
    amps = jnp.concatenate([amps, near], axis=0)
    two = swap(amps, "col", 8, 2)
    place, notes = call(
        place_kernel,
        (virt_irrep, panel, pair_irrep, v_row, p_row),
        [SM, SM, SM, VM, VM],
        (jax.ShapeDtypeStruct((8, CDS * B_PAD), I32), jax.ShapeDtypeStruct((CAP_IN, 128), F32)),
        [pltpu.VMEM((8, B_PAD), F32), turn, pltpu.VMEM((8, 256), I32)],
        4 * 10**8,
        10**5,
    )
    two, place = lax.optimization_barrier((two, place))
    amps = jnp.concatenate([amps, two], axis=0)
    amps = jnp.concatenate([amps, swap(amps, "col", 8, 4)], axis=0)
    sent = call(
        pack_kernel,
        (notes, v_row, place, integrals),
        [VM] * 4,
        jax.ShapeDtypeStruct((rows, A_PAD), BF),
        [
            pltpu.VMEM((rows, CDS * B_PAD), BF),
            pltpu.VMEM((CDS * B_PAD, A_PAD), BF),
            turn,
        ],
        2 * rows * CDS * B_PAD * A_PAD,
        2 * B_COLS * CDS * A_ROWS,
    )
    last = pl.BlockSpec((rows, 128), lambda n: (0, A_PAD // 128 - 1))
    sent = pl.pallas_call(
        note_kernel,
        out_shape=jax.ShapeDtypeStruct((rows, A_PAD), BF),
        grid=(1,),
        in_specs=[
            pl.BlockSpec((CAP_IN, 128), lambda n: (0, 0)),
            pl.BlockSpec((1, 128), lambda n: (0, 0)),
            pl.BlockSpec((128, CDS), lambda n: (0, 0)),
            last,
        ],
        out_specs=last,
        scratch_shapes=[pltpu.VMEM((CAP_IN, 128), F32), pltpu.VMEM((128, CDS), F32)],
        input_output_aliases={3: 0},
        compiler_params=pltpu.CompilerParams(vmem_limit_bytes=VMEM_LIMIT),
        cost_estimate=pl.CostEstimate(flops=10**7, bytes_accessed=4 * rows * 128, transcendentals=0),
    )(notes, p_row, amps, sent)
    held = lax.all_to_all(sent.reshape(LAYERS, CAP_IN, A_PAD), "depth", 0, 0, tiled=True)
    shared = held[:, :, A_ROWS : A_ROWS + 2 * CDS].reshape(LAYERS, CAP_IN, 2, CDS)
    shared = shared.transpose(2, 1, 0, 3).reshape(2, CAP_IN, LAYERS * CDS)
    over = jnp.max(shared[1, 1, :].astype(F32)) > 0.5

    def packed(shared, held, amps):
        part = call(
            compute_kernel,
            (v_row, p_row, shared, held.reshape(rows, A_PAD)),
            [VM] * 4,
            jax.ShapeDtypeStruct((out_rows, A_PAD), F32),
            [
                pltpu.VMEM((PER * 64, 4 * CAP_IN), BF),
                pltpu.VMEM((PER * 256, A_PAD), BF),
                pltpu.VMEM((out_rows, PER * 256), BF),
                pltpu.VMEM((out_rows, 128), BF),
                turn,
            ],
            2 * PER * 256 * A_PAD * (out_rows + 4 * CAP_IN),
            2 * rows * A_PAD,
        )
        turned = [list(range(LAYERS - 1, -1, -1))]
        part = part.reshape(LAYERS, CAP_OUT, A_PAD)
        back = lax.all_to_all(part, "depth", 0, 0, tiled=True, axis_index_groups=turned)
        return call(
            unpack_kernel,
            (pair_irrep, v_row, back.reshape(out_rows, A_PAD)),
            [SM, VM, VM],
            jax.ShapeDtypeStruct((B_COLS, OWN_IJ * A_ROWS), F32),
            [
                pltpu.VMEM((OWN_IJ * B_PAD, out_rows), BF),
                pltpu.VMEM((out_rows, A_PAD), BF),
                pltpu.VMEM((out_rows, A_PAD), BF),
                pltpu.SMEM((8,), I32),
                turn,
            ],
            4 * OWN_IJ * B_PAD * out_rows * A_PAD,
            4 * B_COLS * OWN_IJ * A_ROWS,
        )

    def general(shared, held, amps):
        return dense(amps, shared, integrals, virt_irrep, pair_irrep)

    return lax.cond(over, general, packed, shared, held, amps)


def solution(mesh):
    return jax.shard_map(
        body,
        mesh=mesh,
        in_specs=(
            P(("row", "col"), "depth"),
            P("col", ("row", "depth")),
            P(),
            P(),
            P("depth"),
            P("depth"),
        ),
        out_specs=P("col", ("row", "depth")),
        check_vma=False,
    )
```

```python
import functools

import jax
import jax.numpy as jnp
from jax import lax
from jax.experimental import pallas as pl
from jax.experimental.pallas import tpu as pltpu
from jax.sharding import PartitionSpec as P

NV = 1200
LAYERS = 16
A_ROWS = 600
B_COLS = 150
A_PAD = 640
B_PAD = 160
CDS = 16
OWN_IJ = 8
CAP_IN = 40
CAP_OUT = 24
CAP_LOW = 20
HALF = 80
PER = 10
TURN = 1280
META = A_ROWS - 512
BF = jnp.bfloat16
F32 = jnp.float32
I32 = jnp.int32
VMEM_LIMIT = 20 * 1024 * 1024
DN = (((1,), (0,)), ((), ()))


def iota(shape, dim):
    return lax.broadcasted_iota(I32, shape, dim)


def dot(x, y):
    return lax.dot_general(x, y, DN, preferred_element_type=F32)


def to_col(row):
    size = row.shape[1]
    eye = iota((size, size), 0) == iota((size, size), 1)
    spread = jnp.where(eye, jnp.broadcast_to(row.astype(F32), (size, size)), 0.0)
    return jnp.sum(spread, axis=1, keepdims=True).astype(I32)


def ones(mask):
    return jnp.where(mask, 1.0, 0.0)


def ranks(b_row):
    key_row = b_row * 256 + iota(b_row.shape, 1)
    key_col = to_col(key_row)
    rank_row = jnp.sum(ones(key_col < key_row), axis=0, keepdims=True).astype(I32)
    rank_col = jnp.sum(ones(key_row < key_col), axis=1, keepdims=True).astype(I32)
    return rank_row, rank_col, jnp.right_shift(key_col, 8)


def irreps(v_ref, turn):
    turn[:, 0:NV] = jnp.broadcast_to(v_ref[...], (8, NV))
    turn[:, NV:] = jnp.zeros((8, TURN - NV), I32)
    whole = turn[...]
    a_at = lax.axis_index("row") * A_ROWS
    b_at = lax.axis_index("col") * B_COLS
    a_row = pltpu.roll(whole, TURN - a_at, 1)[0:1, 0:A_PAD]
    b_row = pltpu.roll(whole, TURN - b_at, 1)[0:1, 0:B_PAD]
    a_row = jnp.where(iota((1, A_PAD), 1) < A_ROWS, a_row, 64)
    return a_row, jnp.where(iota((1, B_PAD), 1) < B_COLS, b_row, 16)


def class_counts(labels):
    count = [sum((label == y).astype(I32) for label in labels) for y in range(8)]
    order = [sum([(labels[k] == labels[j]).astype(I32) for k in range(j)], jnp.int32(0)) for j in range(len(labels))]
    return count, order


def slots(pair_ref):
    p_row = pair_ref[...]
    p_col = to_col(p_row)
    square = (128, 128)
    alike = p_row == p_col
    row = jnp.sum(ones(jnp.logical_and(alike, iota(square, 0) < iota(square, 1))), axis=0, keepdims=True)
    col = jnp.sum(ones(jnp.logical_and(alike, iota(square, 1) < iota(square, 0))), axis=1, keepdims=True)
    return row.astype(I32), col.astype(I32), p_col


def place_kernel(virt, panel, pair, v_ref, pair_ref, q_ref, m_ref, s_ref, turn, each):
    me = lax.axis_index("depth")
    _, b_row = irreps(v_ref, turn)
    g = [virt[panel[j]] ^ virt[panel[CDS + j]] for j in range(CDS)]
    rank_row, rank_col, b_col = ranks(b_row)
    same = jnp.logical_and((rank_row & 15) == (rank_col & 15), rank_col < rank_row)
    diff = b_col ^ b_row
    before = [jnp.sum(ones(jnp.logical_and(same, diff == y)), axis=0, keepdims=True) for y in range(8)]
    count, order = class_counts(g)
    count = [c.astype(F32) for c in count]
    for x in range(8):
        s_ref[x : x + 1, :] = sum(count[y ^ x] * before[y] for y in range(8))
    first = (rank_row & 15) * CAP_IN
    for j in range(CDS):
        place = s_ref[pl.ds(g[j], 1), :] + order[j].astype(F32)
        q_ref[0:1, j * B_PAD : (j + 1) * B_PAD] = first + place.astype(I32)

    own = [pair[me * OWN_IJ + j] for j in range(OWN_IJ)]
    for c in range(8):
        each[c : c + 1, 0:B_COLS] = turn[0:1, c * B_COLS : (c + 1) * B_COLS]
    of_col = each[:, 0:B_COLS]
    chunk = jnp.maximum(15 - iota((8, 128), 1), 0)
    start = jnp.zeros((8, 1), I32)
    dealt = []
    for h in range(8):
        end = start + jnp.sum(ones(of_col == h), axis=1, keepdims=True).astype(I32)
        dealt.append((jnp.right_shift(end + chunk, 4) - jnp.right_shift(start + chunk, 4)).astype(F32))
        start = end
    over = jnp.zeros((8, 128), F32)
    results = [c.astype(F32) for c in class_counts(own)[0]]
    for x in range(8):
        stacked = sum(count[y ^ x] * dealt[y] for y in range(8))
        back = sum(results[y ^ x] * dealt[y] for y in range(8))
        wrong = jnp.logical_or(stacked > CAP_IN, back > CAP_OUT)
        over = jnp.maximum(over, jnp.where(wrong, 2.0, ones(back > CAP_LOW)))
    slot_row, _, _ = slots(pair_ref)
    crowd = jnp.max(slot_row, axis=1, keepdims=True) >= CAP_IN
    over = jnp.maximum(jnp.max(over, axis=(0, 1), keepdims=True), jnp.where(crowd, 2.0, 0.0))
    lane = iota((1, CDS), 1)
    m_ref[...] = jnp.zeros_like(m_ref)
    m_ref[0:1, META + CDS : META + 2 * CDS] = sum(jnp.where(lane == j, g[j], 0) for j in range(CDS)).astype(F32)
    m_ref[1:2, META + CDS : META + 2 * CDS] = jnp.broadcast_to(over, (1, CDS))


def pack_kernel(g_ref, v_ref, q_ref, eri_ref, x_ref, hot, masked, turn):
    a_row, b_row = irreps(v_ref, turn)
    b_col = to_col(b_row)
    rows = LAYERS * CAP_IN
    for t in range(CDS * B_PAD // 512):
        at = slice(t * 512, (t + 1) * 512)
        hot[:, at] = ones(iota((rows, 512), 0) == q_ref[0:1, at]).astype(BF)
    masked[:, 512:A_PAD] = jnp.zeros((CDS * B_PAD, 128), BF)
    for j in range(CDS):
        masked[(j + 1) * B_PAD - 16 : (j + 1) * B_PAD, 0:512] = jnp.zeros((16, 512), BF)
    ab = (b_col ^ a_row)[:B_COLS, :A_ROWS].astype(F32).astype(BF)
    for j in range(CDS):
        slab = eri_ref[:, j * A_ROWS : (j + 1) * A_ROWS]
        label = g_ref[0:1, META + CDS + j : META + CDS + j + 1].astype(BF)
        masked[j * B_PAD : j * B_PAD + B_COLS, 0:A_ROWS] = jnp.where(ab == label, slab, jnp.zeros_like(slab))
    for n, w in ((0, 256), (256, 256), (512, 128)):
        x_ref[:, n : n + w] = dot(hot[...], masked[:, n : n + w]).astype(BF)


def note_kernel(g_ref, pair_ref, amp_ref, x_in, x_ref, m_ref, amps):
    slot_row, _, p_col = slots(pair_ref)
    g_row = g_ref[0:1, META + CDS : META + 2 * CDS].astype(I32)
    for k in range(16):
        block = (lax.axis_index("row") ^ (k & 1)) * 8 + (lax.axis_index("col") ^ (k >> 1))
        amps[pl.ds(pl.multiple_of(block * 8, 8), 8), :] = amp_ref[k * 8 : (k + 1) * 8, :].astype(F32)
    allowed = jnp.where(p_col == g_row, amps[...], 0.0).astype(BF)
    in_slot = ones(iota((CAP_IN, 128), 0) == slot_row).astype(BF)
    m_ref[...] = g_ref[...]
    m_ref[:, META : META + CDS] = dot(in_slot, allowed)
    note = m_ref[...]
    whole = jnp.concatenate([note] * LAYERS, axis=0)
    x_ref[...] = (x_in[...].astype(F32) + whole).astype(BF)


def compute_kernel(v_ref, pair_ref, y_ref, x_ref, pair_out, over_ref, hot, eri, amp, hot2, turn, notes, tail, stage):
    me = lax.axis_index("depth")
    tail[...] = y_ref[:, A_PAD - 128 : A_PAD].astype(F32)
    for c in range(LAYERS):
        at = slice(c * CDS, (c + 1) * CDS)
        notes[0:CAP_IN, at] = tail[c * CAP_IN : (c + 1) * CAP_IN, META : META + CDS]
        notes[CAP_IN : CAP_IN + 8, at] = tail[c * CAP_IN : c * CAP_IN + 8, META + CDS : META + 2 * CDS]
    over_ref[0] = jnp.max(notes[CAP_IN + 1 : CAP_IN + 2, :]).astype(I32)
    a_row, b_row = irreps(v_ref, turn)
    rank_row, _, _ = ranks(b_row)
    beta = []
    for i in range(PER):
        mine = rank_row == i * LAYERS + me
        beta.append(jnp.sum(jnp.where(mine, b_row, 0).astype(F32), axis=1, keepdims=True).astype(I32))

    g_row = notes[CAP_IN : CAP_IN + 1, :].astype(I32)
    g_col = to_col(g_row)
    wide = (256, 256)
    same = jnp.right_shift(iota(wide, 0), 4) == jnp.right_shift(iota(wide, 1), 4)
    earlier = jnp.logical_and(same, iota(wide, 1) < iota(wide, 0))
    order = jnp.sum(ones(jnp.logical_and(earlier, g_row == g_col)), axis=1, keepdims=True)
    lane = iota((1, 128), 1)
    part, label = jnp.right_shift(lane, 3), lane & 7
    own = sum(jnp.where(part == i, beta[i], 0) for i in range(PER))
    wanted = (label ^ own) ^ g_col
    seen = sum(ones(jnp.logical_and(part > i, wanted == beta[i])) for i in range(PER - 1))
    count = dot(ones(same).astype(BF), ones(g_col == label).astype(BF))
    square = (128, 128)
    by_part = ones(jnp.right_shift(iota(square, 0), 3) == iota(square, 1)).astype(BF)
    place = dot((seen * count).astype(BF), by_part) + order
    rows = iota((256, 1), 0)
    place = place.astype(I32) + (jnp.right_shift(rows, 4) & 3) * CAP_IN

    four = 4 * CAP_IN
    sym = [a_row ^ beta[i] for i in range(PER)]
    for k in range(4):
        at = slice(k * 64, (k + 1) * 64)
        for i in range(PER):
            hot[i * 64 : (i + 1) * 64, :] = ones(iota((64, four), 1) == place[at, i : i + 1]).astype(BF)
        for n, w in ((0, 256), (256, 256), (512, 128)):
            got = dot(hot[...], y_ref[k * four : (k + 1) * four, n : n + w])
            for i in range(PER):
                keep = sym[i][:, n : n + w] == g_col[at, :]
                eri[i * 256 + k * 64 : i * 256 + (k + 1) * 64, n : n + w] = jnp.where(
                    keep, got[i * 64 : (i + 1) * 64, :], 0.0
                ).astype(BF)

    p_row = pair_ref[...]
    _, slot_col, p_col = slots(pair_ref)
    from_slot = ones(iota((128, CAP_IN), 1) == slot_col).astype(BF)
    allowed = jnp.where(p_col == g_row, dot(from_slot, notes[0:CAP_IN, :].astype(BF)), 0.0).astype(BF)
    same2 = jnp.right_shift(iota(square, 0), 3) == jnp.right_shift(iota(square, 1), 3)
    earlier2 = jnp.logical_and(same2, iota(square, 0) < iota(square, 1))
    order2 = jnp.sum(ones(jnp.logical_and(earlier2, p_row == p_col)), axis=0, keepdims=True)
    row = iota((128, 1), 0)
    part2, label2 = jnp.right_shift(row, 3), row & 7
    own2 = sum(jnp.where(part2 == i, beta[i], 0) for i in range(PER))
    wanted2 = (label2 ^ own2) ^ p_row
    seen2 = sum(ones(jnp.logical_and(part2 > i, wanted2 == beta[i])) for i in range(PER - 1))
    count2 = dot(ones(label2 == p_row).astype(BF), ones(same2).astype(BF))
    short = (16, 128)
    by_part2 = ones(jnp.right_shift(iota(short, 1), 3) == iota(short, 0)).astype(BF)
    place2 = dot(by_part2, (seen2 * count2).astype(BF)) + order2
    place2 = place2.astype(I32) + (LAYERS - 1 - jnp.right_shift(iota((1, 128), 1), 3)) * CAP_OUT
    out_rows = LAYERS * CAP_OUT
    for i in range(PER):
        hot2[...] = ones(iota((out_rows, 128), 0) == place2[i : i + 1, :]).astype(BF)
        amp[:, i * 256 : (i + 1) * 256] = dot(hot2[...], allowed).astype(BF)
    for n, w in ((0, 256), (256, 256), (512, 128)):
        got = dot(amp[...], eri[:, n : n + w])
        x_ref[:, n : n + w] = got
        high = got.astype(BF).astype(F32)
        low = got - high
        for k in range(LAYERS):
            at = slice(k * CAP_OUT, k * CAP_OUT + CAP_LOW)
            stage[k * CAP_IN : k * CAP_IN + CAP_LOW, 0:w] = high[at, :]
            stage[k * CAP_IN + CAP_LOW : (k + 1) * CAP_IN, 0:w] = low[at, :]
        pair_out[:, n : n + w] = stage[:, 0:w].astype(BF)


def unpack_kernel(stride, gap, pair, v_ref, y_ref, o_ref, hot, both, sym, j_ref, turn):
    step = pl.program_id(0)
    me = lax.axis_index("depth")
    labels = [pair[me * OWN_IJ + j] for j in range(OWN_IJ)]
    width = hot.shape[1]

    @pl.when(step == 0)
    def _():
        a_row, b_row = irreps(v_ref, turn)
        count, order = class_counts(labels)
        for y in range(8):
            j_ref[y] = count[y]
        rank_row, rank_col, b_col = ranks(b_row)
        same = jnp.logical_and((rank_row & 15) == (rank_col & 15), rank_row < rank_col)
        diff = b_col ^ b_row
        before = [jnp.sum(ones(jnp.logical_and(same, diff == y)), axis=1, keepdims=True) for y in range(8)]
        first = (LAYERS - 1 - (rank_col & 15)) * stride
        for j in range(OWN_IJ):
            place = sum(j_ref[y ^ labels[j]].astype(F32) * before[y] for y in range(8)) + order[j].astype(F32)
            place = first + place.astype(I32)
            for t in range(2):
                mine = place[t * HALF : (t + 1) * HALF, :]
                lane = iota((HALF, width), 1)
                at = (t * OWN_IJ + j) * HALF
                hot[at : at + HALF, :] = ones(jnp.logical_or(lane == mine, lane == mine + gap)).astype(BF)
        sym[...] = b_col ^ a_row
        if y_ref.dtype == F32:
            whole = y_ref[...]
            top = whole.astype(BF)
            both[0:gap, :] = top
            both[gap : 2 * gap, :] = (whole - top.astype(F32)).astype(BF)

    terms = both if y_ref.dtype == F32 else y_ref
    rows = OWN_IJ * HALF
    of_step = hot[pl.ds(pl.multiple_of(step * rows, rows), rows), :]
    ab = sym[pl.ds(pl.multiple_of(step * HALF, HALF), HALF), :]
    for n, w, real in ((0, 256, 256), (256, 256, 256), (512, 128, A_ROWS - 512)):
        got = dot(of_step, terms[:, n : n + w])
        for j in range(OWN_IJ):
            part = jnp.where(ab[:, n : n + w] == labels[j], got[j * HALF : (j + 1) * HALF, :], 0.0)
            o_ref[:, j * A_ROWS + n : j * A_ROWS + n + real] = part[:, :real]


VM = pl.BlockSpec(memory_space=pltpu.VMEM)
SM = pl.BlockSpec(memory_space=pltpu.SMEM)


def call(kernel, args, specs, out, scratch, flops, moved, outs=VM):
    return pl.pallas_call(
        kernel,
        out_shape=out,
        in_specs=specs,
        out_specs=outs,
        scratch_shapes=scratch,
        compiler_params=pltpu.CompilerParams(vmem_limit_bytes=VMEM_LIMIT),
        cost_estimate=pl.CostEstimate(flops=flops, bytes_accessed=moved, transcendentals=0),
    )(*args)


def dense(rows, held, integrals, virt_irrep, pair_irrep):
    rows = rows.reshape(LAYERS, OWN_IJ, CDS)
    at = jnp.arange(LAYERS)
    at = (lax.axis_index("row") ^ (at >> 3)) + 2 * (lax.axis_index("col") ^ (at & 7))
    amps = jnp.take(rows, at, axis=0).reshape(1, LAYERS * OWN_IJ, CDS)
    amps = jnp.broadcast_to(amps, (LAYERS, LAYERS * OWN_IJ, CDS))
    amps = lax.all_to_all(amps, "depth", 0, 0, tiled=True).transpose(1, 0, 2).reshape(-1, LAYERS * CDS)
    pair_sym = held[:, 0, A_ROWS + CDS : A_ROWS + 2 * CDS].reshape(-1).astype(I32)
    allowed = jnp.where(pair_irrep[:, None] == pair_sym[None, :], amps, jnp.zeros_like(amps))
    share = B_PAD // LAYERS
    padded = jnp.pad(integrals, ((0, B_PAD - B_COLS), (0, 0))).reshape(LAYERS, share, CDS * A_ROWS)
    piece = lax.all_to_all(padded, "depth", 0, 0, tiled=True).reshape(LAYERS, share, CDS, A_ROWS)
    full = jnp.einsum("jsc,sbca->jba", allowed.reshape(-1, LAYERS, CDS), piece, preferred_element_type=F32)
    back = lax.all_to_all(full, "depth", 0, 0, tiled=True).reshape(LAYERS, OWN_IJ, share, A_ROWS)
    mine = back.transpose(0, 2, 1, 3).reshape(B_PAD, OWN_IJ, A_ROWS)[:B_COLS]
    irrep_a = lax.dynamic_slice_in_dim(virt_irrep, lax.axis_index("row") * A_ROWS, A_ROWS, 0)
    irrep_b = lax.dynamic_slice_in_dim(virt_irrep, lax.axis_index("col") * B_COLS, B_COLS, 0)
    irrep_ij = lax.dynamic_slice_in_dim(pair_irrep, lax.axis_index("depth") * OWN_IJ, OWN_IJ, 0)
    ab_sym = jnp.bitwise_xor(irrep_b[:, None], irrep_a[None, :])
    mask = irrep_ij[None, :, None] == ab_sym[:, None, :]
    return jnp.where(mask, mine, jnp.float32(0.0)).reshape(B_COLS, OWN_IJ * A_ROWS)


def swap(array, axis, size, step):
    return lax.ppermute(array, axis, [(d, d ^ step) for d in range(size)])


def body(amplitudes, integrals, virt_irrep, pair_irrep, panel_c, panel_d):
    rows = LAYERS * CAP_IN
    out_rows = LAYERS * CAP_OUT
    p_row = pair_irrep[None, :]
    turn = pltpu.VMEM((8, TURN), I32)
    amps = jnp.concatenate([amplitudes, swap(amplitudes, "row", 2, 1)], axis=0)
    amps, virt_irrep, panel_c, panel_d = lax.optimization_barrier((amps, virt_irrep, panel_c, panel_d))
    near = swap(amps, "col", 8, 1)
    v_row = virt_irrep[None, :]
    panel = jnp.concatenate([panel_c, panel_d])
    near, v_row, panel = lax.optimization_barrier((near, v_row, panel))
    amps = jnp.concatenate([amps, near], axis=0)
    two = swap(amps, "col", 8, 2)
    place, notes = call(
        place_kernel,
        (virt_irrep, panel, pair_irrep, v_row, p_row),
        [SM, SM, SM, VM, VM],
        (jax.ShapeDtypeStruct((8, CDS * B_PAD), I32), jax.ShapeDtypeStruct((CAP_IN, 128), F32)),
        [pltpu.VMEM((8, B_PAD), F32), turn, pltpu.VMEM((8, 256), I32)],
        4 * 10**8,
        10**5,
        (VM, VM),
    )
    two, place = lax.optimization_barrier((two, place))
    amps = jnp.concatenate([amps, two], axis=0)
    amps = jnp.concatenate([amps, swap(amps, "col", 8, 4)], axis=0)
    sent = call(
        pack_kernel,
        (notes, v_row, place, integrals),
        [VM] * 4,
        jax.ShapeDtypeStruct((rows, A_PAD), BF),
        [
            pltpu.VMEM((rows, CDS * B_PAD), BF),
            pltpu.VMEM((CDS * B_PAD, A_PAD), BF),
            turn,
        ],
        2 * rows * CDS * B_PAD * A_PAD,
        2 * B_COLS * CDS * A_ROWS,
    )
    last = pl.BlockSpec((rows, 128), lambda n: (0, A_PAD // 128 - 1))
    sent = pl.pallas_call(
        note_kernel,
        out_shape=jax.ShapeDtypeStruct((rows, A_PAD), BF),
        grid=(1,),
        in_specs=[
            pl.BlockSpec((CAP_IN, 128), lambda n: (0, 0)),
            pl.BlockSpec((1, 128), lambda n: (0, 0)),
            pl.BlockSpec((128, CDS), lambda n: (0, 0)),
            last,
        ],
        out_specs=last,
        scratch_shapes=[pltpu.VMEM((CAP_IN, 128), F32), pltpu.VMEM((128, CDS), F32)],
        input_output_aliases={3: 0},
        compiler_params=pltpu.CompilerParams(vmem_limit_bytes=VMEM_LIMIT),
        cost_estimate=pl.CostEstimate(flops=10**7, bytes_accessed=4 * rows * 128, transcendentals=0),
    )(notes, p_row, amps, sent)
    held = lax.all_to_all(sent.reshape(LAYERS, CAP_IN, A_PAD), "depth", 0, 0, tiled=True)
    part, terms, over = call(
        compute_kernel,
        (v_row, p_row, held.reshape(rows, A_PAD)),
        [VM] * 3,
        (
            jax.ShapeDtypeStruct((out_rows, A_PAD), F32),
            jax.ShapeDtypeStruct((rows, A_PAD), BF),
            jax.ShapeDtypeStruct((1,), I32),
        ),
        [
            pltpu.VMEM((PER * 64, 4 * CAP_IN), BF),
            pltpu.VMEM((PER * 256, A_PAD), BF),
            pltpu.VMEM((out_rows, PER * 256), BF),
            pltpu.VMEM((out_rows, 128), BF),
            turn,
            pltpu.VMEM((CAP_IN + 8, LAYERS * CDS), F32),
            pltpu.VMEM((rows, 128), F32),
            pltpu.VMEM((rows, 256), F32),
        ],
        2 * PER * 256 * A_PAD * (out_rows + 4 * CAP_IN),
        2 * rows * A_PAD,
        (VM, VM, SM),
    )

    turned = [list(range(LAYERS - 1, -1, -1))]

    def finish(array, stride, gap):
        chunks = array.reshape(LAYERS, stride, A_PAD)
        back = lax.all_to_all(chunks, "depth", 0, 0, tiled=True, axis_index_groups=turned)
        back = back.reshape(array.shape)
        width = 2 * gap if array.dtype == F32 else array.shape[0]
        whole = lambda shape: pl.BlockSpec(shape, lambda t: (0, 0))
        return pl.pallas_call(
            functools.partial(unpack_kernel, stride, gap),
            out_shape=jax.ShapeDtypeStruct((B_COLS, OWN_IJ * A_ROWS), F32),
            grid=(2,),
            in_specs=[SM, whole((1, NV)), whole(array.shape)],
            out_specs=pl.BlockSpec((HALF, OWN_IJ * A_ROWS), lambda t: (t, 0)),
            scratch_shapes=[
                pltpu.VMEM((2 * OWN_IJ * HALF, width), BF),
                pltpu.VMEM((width if array.dtype == F32 else 16, A_PAD), BF),
                pltpu.VMEM((B_PAD, A_PAD), I32),
                pltpu.SMEM((8,), I32),
                turn,
            ],
            compiler_params=pltpu.CompilerParams(vmem_limit_bytes=VMEM_LIMIT),
            cost_estimate=pl.CostEstimate(
                flops=4 * OWN_IJ * HALF * width * A_PAD,
                bytes_accessed=4 * B_COLS * OWN_IJ * A_ROWS,
                transcendentals=0,
            ),
        )(pair_irrep, v_row, back)

    def usual(part, terms, held, amps):
        return finish(terms, CAP_IN, CAP_LOW)

    def fuller(part, terms, held, amps):
        return finish(part, CAP_OUT, out_rows)

    def general(part, terms, held, amps):
        return dense(amps, held, integrals, virt_irrep, pair_irrep)

    return lax.switch(over[0], (usual, fuller, general), part, terms, held, amps)


def solution(mesh):
    return jax.shard_map(
        body,
        mesh=mesh,
        in_specs=(
            P(("row", "col"), "depth"),
            P("col", ("row", "depth")),
            P(),
            P(),
            P("depth"),
            P("depth"),
        ),
        out_specs=P("col", ("row", "depth")),
        check_vma=False,
    )
```

```python
import jax
import jax.numpy as jnp
from jax import lax
from jax.experimental import pallas as pl
from jax.experimental.pallas import tpu as pltpu
from jax.sharding import PartitionSpec as P

NV = 1200
LAYERS = 16
A_ROWS = 600
B_COLS = 150
A_PAD = 640
B_PAD = 160
CDS = 16
OWN_IJ = 8
CAP_IN = 40
CAP_OUT = 24
CAP_LOW = 20
HALF = 80
PER = 10
TURN = 1280
META = A_ROWS - 512
BF = jnp.bfloat16
F32 = jnp.float32
I32 = jnp.int32
VMEM_LIMIT = 20 * 1024 * 1024
DN = (((1,), (0,)), ((), ()))


def iota(shape, dim):
    return lax.broadcasted_iota(I32, shape, dim)


def dot(x, y):
    return lax.dot_general(x, y, DN, preferred_element_type=F32)


def to_col(row):
    size = row.shape[1]
    eye = iota((size, size), 0) == iota((size, size), 1)
    spread = jnp.where(eye, jnp.broadcast_to(row.astype(F32), (size, size)), 0.0)
    return jnp.sum(spread, axis=1, keepdims=True).astype(I32)


def ones(mask):
    return jnp.where(mask, 1.0, 0.0)


def ranks(b_row):
    key_row = b_row * 256 + iota(b_row.shape, 1)
    key_col = to_col(key_row)
    rank_row = jnp.sum(ones(key_col < key_row), axis=0, keepdims=True).astype(I32)
    rank_col = jnp.sum(ones(key_row < key_col), axis=1, keepdims=True).astype(I32)
    return rank_row, rank_col, jnp.right_shift(key_col, 8)


def irreps(v_ref, turn):
    turn[:, 0:NV] = jnp.broadcast_to(v_ref[...], (8, NV))
    turn[:, NV:] = jnp.zeros((8, TURN - NV), I32)
    whole = turn[...]
    a_at = lax.axis_index("row") * A_ROWS
    b_at = lax.axis_index("col") * B_COLS
    a_row = pltpu.roll(whole, TURN - a_at, 1)[0:1, 0:A_PAD]
    b_row = pltpu.roll(whole, TURN - b_at, 1)[0:1, 0:B_PAD]
    a_row = jnp.where(iota((1, A_PAD), 1) < A_ROWS, a_row, 64)
    return a_row, jnp.where(iota((1, B_PAD), 1) < B_COLS, b_row, 16)


def own_irreps(b_row):
    me = lax.axis_index("depth")
    rank_row, _, _ = ranks(b_row)
    beta = []
    for i in range(PER):
        mine = rank_row == i * LAYERS + me
        beta.append(jnp.sum(jnp.where(mine, b_row, 0).astype(F32), axis=1, keepdims=True).astype(I32))
    return beta


def class_counts(labels):
    count = [sum((label == y).astype(I32) for label in labels) for y in range(8)]
    order = [sum([(labels[k] == labels[j]).astype(I32) for k in range(j)], jnp.int32(0)) for j in range(len(labels))]
    return count, order


def slots(pair_ref):
    p_row = pair_ref[...]
    p_col = to_col(p_row)
    square = (128, 128)
    alike = p_row == p_col
    row = jnp.sum(ones(jnp.logical_and(alike, iota(square, 0) < iota(square, 1))), axis=0, keepdims=True)
    col = jnp.sum(ones(jnp.logical_and(alike, iota(square, 1) < iota(square, 0))), axis=1, keepdims=True)
    return row.astype(I32), col.astype(I32), p_col


def place_kernel(virt, panel, pair, v_ref, pair_ref, q_ref, m_ref, s_ref, turn, each):
    me = lax.axis_index("depth")
    _, b_row = irreps(v_ref, turn)
    g = [virt[panel[j]] ^ virt[panel[CDS + j]] for j in range(CDS)]
    rank_row, rank_col, b_col = ranks(b_row)
    same = jnp.logical_and((rank_row & 15) == (rank_col & 15), rank_col < rank_row)
    diff = b_col ^ b_row
    before = [jnp.sum(ones(jnp.logical_and(same, diff == y)), axis=0, keepdims=True) for y in range(8)]
    count, order = class_counts(g)
    count = [c.astype(F32) for c in count]
    for x in range(8):
        s_ref[x : x + 1, :] = sum(count[y ^ x] * before[y] for y in range(8))
    first = (rank_row & 15) * CAP_IN
    for j in range(CDS):
        place = s_ref[pl.ds(g[j], 1), :] + order[j].astype(F32)
        q_ref[0:1, j * B_PAD : (j + 1) * B_PAD] = first + place.astype(I32)

    own = [pair[me * OWN_IJ + j] for j in range(OWN_IJ)]
    for c in range(8):
        each[c : c + 1, 0:B_COLS] = turn[0:1, c * B_COLS : (c + 1) * B_COLS]
    of_col = each[:, 0:B_COLS]
    chunk = jnp.maximum(15 - iota((8, 128), 1), 0)
    start = jnp.zeros((8, 1), I32)
    dealt = []
    for h in range(8):
        end = start + jnp.sum(ones(of_col == h), axis=1, keepdims=True).astype(I32)
        dealt.append((jnp.right_shift(end + chunk, 4) - jnp.right_shift(start + chunk, 4)).astype(F32))
        start = end
    over = jnp.zeros((8, 128), F32)
    results = [c.astype(F32) for c in class_counts(own)[0]]
    for x in range(8):
        stacked = sum(count[y ^ x] * dealt[y] for y in range(8))
        back = sum(results[y ^ x] * dealt[y] for y in range(8))
        wrong = jnp.logical_or(stacked > CAP_IN, back > CAP_OUT)
        over = jnp.maximum(over, jnp.where(wrong, 2.0, ones(back > CAP_LOW)))
    slot_row, _, _ = slots(pair_ref)
    crowd = jnp.max(slot_row, axis=1, keepdims=True) >= CAP_IN
    over = jnp.maximum(jnp.max(over, axis=(0, 1), keepdims=True), jnp.where(crowd, 2.0, 0.0))
    lane = iota((1, CDS), 1)
    m_ref[...] = jnp.zeros_like(m_ref)
    m_ref[0:1, META + CDS : META + 2 * CDS] = sum(jnp.where(lane == j, g[j], 0) for j in range(CDS)).astype(F32)
    m_ref[1:2, META + CDS : META + 2 * CDS] = jnp.broadcast_to(over, (1, CDS))


def pack_kernel(g_ref, v_ref, q_ref, eri_ref, x_ref, hot, masked, turn):
    a_row, b_row = irreps(v_ref, turn)
    b_col = to_col(b_row)
    rows = LAYERS * CAP_IN
    for t in range(CDS * B_PAD // 512):
        at = slice(t * 512, (t + 1) * 512)
        hot[:, at] = ones(iota((rows, 512), 0) == q_ref[0:1, at]).astype(BF)
    masked[:, 512:A_PAD] = jnp.zeros((CDS * B_PAD, 128), BF)
    for j in range(CDS):
        masked[(j + 1) * B_PAD - 16 : (j + 1) * B_PAD, 0:512] = jnp.zeros((16, 512), BF)
    ab = (b_col ^ a_row)[:B_COLS, :A_ROWS].astype(F32).astype(BF)
    for j in range(CDS):
        slab = eri_ref[:, j * A_ROWS : (j + 1) * A_ROWS]
        label = g_ref[0:1, META + CDS + j : META + CDS + j + 1].astype(BF)
        masked[j * B_PAD : j * B_PAD + B_COLS, 0:A_ROWS] = jnp.where(ab == label, slab, jnp.zeros_like(slab))
    for n, w in ((0, 256), (256, 256), (512, 128)):
        x_ref[:, n : n + w] = dot(hot[...], masked[:, n : n + w]).astype(BF)


def note_kernel(g_ref, pair_ref, amp_ref, x_in, x_ref, m_ref, amps):
    slot_row, _, p_col = slots(pair_ref)
    g_row = g_ref[0:1, META + CDS : META + 2 * CDS].astype(I32)
    for k in range(16):
        apart = (k >> 1 & 1) * 4 + (k >> 2 & 1) + (k >> 3) * 2
        block = (lax.axis_index("row") ^ (k & 1)) * 8 + (lax.axis_index("col") ^ apart)
        amps[pl.ds(pl.multiple_of(block * 8, 8), 8), :] = amp_ref[k * 8 : (k + 1) * 8, :].astype(F32)
    allowed = jnp.where(p_col == g_row, amps[...], 0.0).astype(BF)
    in_slot = ones(iota((CAP_IN, 128), 0) == slot_row).astype(BF)
    m_ref[...] = g_ref[...]
    m_ref[:, META : META + CDS] = dot(in_slot, allowed)
    note = m_ref[...]
    whole = jnp.concatenate([note] * LAYERS, axis=0)
    x_ref[...] = (x_in[...].astype(F32) + whole).astype(BF)


def compute_kernel(v_ref, pair_ref, y_ref, x_ref, pair_out, over_ref, hot, eri, amp, hot2, turn, notes, tail, stage):
    me = lax.axis_index("depth")
    tail[...] = y_ref[:, A_PAD - 128 : A_PAD].astype(F32)
    for c in range(LAYERS):
        at = slice(c * CDS, (c + 1) * CDS)
        notes[0:CAP_IN, at] = tail[c * CAP_IN : (c + 1) * CAP_IN, META : META + CDS]
        notes[CAP_IN : CAP_IN + 8, at] = tail[c * CAP_IN : c * CAP_IN + 8, META + CDS : META + 2 * CDS]
    over_ref[0] = jnp.max(notes[CAP_IN + 1 : CAP_IN + 2, :]).astype(I32)
    a_row, b_row = irreps(v_ref, turn)
    beta = own_irreps(b_row)

    g_row = notes[CAP_IN : CAP_IN + 1, :].astype(I32)
    g_col = to_col(g_row)
    wide = (256, 256)
    same = jnp.right_shift(iota(wide, 0), 4) == jnp.right_shift(iota(wide, 1), 4)
    earlier = jnp.logical_and(same, iota(wide, 1) < iota(wide, 0))
    order = jnp.sum(ones(jnp.logical_and(earlier, g_row == g_col)), axis=1, keepdims=True)
    lane = iota((1, 128), 1)
    part, label = jnp.right_shift(lane, 3), lane & 7
    own = sum(jnp.where(part == i, beta[i], 0) for i in range(PER))
    wanted = (label ^ own) ^ g_col
    seen = sum(ones(jnp.logical_and(part > i, wanted == beta[i])) for i in range(PER - 1))
    count = dot(ones(same).astype(BF), ones(g_col == label).astype(BF))
    square = (128, 128)
    by_part = ones(jnp.right_shift(iota(square, 0), 3) == iota(square, 1)).astype(BF)
    place = dot((seen * count).astype(BF), by_part) + order
    rows = iota((256, 1), 0)
    place = place.astype(I32) + (jnp.right_shift(rows, 4) & 3) * CAP_IN

    four = 4 * CAP_IN
    sym = [a_row ^ beta[i] for i in range(PER)]
    for k in range(4):
        at = slice(k * 64, (k + 1) * 64)
        for i in range(PER):
            hot[i * 64 : (i + 1) * 64, :] = ones(iota((64, four), 1) == place[at, i : i + 1]).astype(BF)
        for n, w in ((0, 256), (256, 256), (512, 128)):
            got = dot(hot[...], y_ref[k * four : (k + 1) * four, n : n + w])
            for i in range(PER):
                keep = sym[i][:, n : n + w] == g_col[at, :]
                eri[i * 256 + k * 64 : i * 256 + (k + 1) * 64, n : n + w] = jnp.where(
                    keep, got[i * 64 : (i + 1) * 64, :], 0.0
                ).astype(BF)

    _, slot_col, p_col = slots(pair_ref)
    from_slot = ones(iota((128, CAP_IN), 1) == slot_col).astype(BF)
    allowed = jnp.where(p_col == g_row, dot(from_slot, notes[0:CAP_IN, :].astype(BF)), 0.0).astype(BF)
    p_row = pair_ref[...]
    same2 = jnp.right_shift(iota(square, 0), 3) == jnp.right_shift(iota(square, 1), 3)
    earlier2 = jnp.logical_and(same2, iota(square, 0) < iota(square, 1))
    order2 = jnp.sum(ones(jnp.logical_and(earlier2, p_row == p_col)), axis=0, keepdims=True)
    row = iota((128, 1), 0)
    part2, label2 = jnp.right_shift(row, 3), row & 7
    own2 = sum(jnp.where(part2 == i, beta[i], 0) for i in range(PER))
    wanted2 = (label2 ^ own2) ^ p_row
    seen2 = sum(ones(jnp.logical_and(part2 > i, wanted2 == beta[i])) for i in range(PER - 1))
    count2 = dot(ones(label2 == p_row).astype(BF), ones(same2).astype(BF))
    short = (16, 128)
    by_part2 = ones(jnp.right_shift(iota(short, 1), 3) == iota(short, 0)).astype(BF)
    place2 = dot(by_part2, (seen2 * count2).astype(BF)) + order2
    place2 = place2.astype(I32) + (LAYERS - 1 - jnp.right_shift(iota((1, 128), 1), 3)) * CAP_OUT
    out_rows = LAYERS * CAP_OUT
    for i in range(PER):
        hot2[...] = ones(iota((out_rows, 128), 0) == place2[i : i + 1, :]).astype(BF)
        amp[:, i * 256 : (i + 1) * 256] = dot(hot2[...], allowed).astype(BF)
    for n, w in ((0, 256), (256, 256), (512, 128)):
        got = dot(amp[...], eri[:, n : n + w])
        x_ref[:, n : n + w] = got
        high = got.astype(BF).astype(F32)
        low = got - high
        for k in range(LAYERS):
            at = slice(k * CAP_OUT, k * CAP_OUT + CAP_LOW)
            stage[k * CAP_IN : k * CAP_IN + CAP_LOW, 0:w] = high[at, :]
            stage[k * CAP_IN + CAP_LOW : (k + 1) * CAP_IN, 0:w] = low[at, :]
        pair_out[:, n : n + w] = stage[:, 0:w].astype(BF)


def unpack_tables(stride, gap, pair, v_ref, hot, sym, j_ref, turn):
    me = lax.axis_index("depth")
    labels = [pair[me * OWN_IJ + j] for j in range(OWN_IJ)]
    width = hot.shape[1]
    a_row, b_row = irreps(v_ref, turn)
    count, order = class_counts(labels)
    for y in range(8):
        j_ref[y] = count[y]
    rank_row, rank_col, b_col = ranks(b_row)
    same = jnp.logical_and((rank_row & 15) == (rank_col & 15), rank_row < rank_col)
    diff = b_col ^ b_row
    before = [jnp.sum(ones(jnp.logical_and(same, diff == y)), axis=1, keepdims=True) for y in range(8)]
    first = (LAYERS - 1 - (rank_col & 15)) * stride
    for j in range(OWN_IJ):
        place = sum(j_ref[y ^ labels[j]].astype(F32) * before[y] for y in range(8)) + order[j].astype(F32)
        place = first + place.astype(I32)
        for t in range(2):
            mine = place[t * HALF : (t + 1) * HALF, :]
            lane = iota((HALF, width), 1)
            at = (t * OWN_IJ + j) * HALF
            hot[at : at + HALF, :] = ones(jnp.logical_or(lane == mine, lane == mine + gap)).astype(BF)
    sym[...] = b_col ^ a_row


def unpack_step(pair, hot, sym, terms, o_ref):
    step = pl.program_id(0)
    me = lax.axis_index("depth")
    rows = OWN_IJ * HALF
    of_step = hot[pl.ds(pl.multiple_of(step * rows, rows), rows), :]
    ab = sym[pl.ds(pl.multiple_of(step * HALF, HALF), HALF), :]
    for n, w, real in ((0, 256, 256), (256, 256, 256), (512, 128, A_ROWS - 512)):
        got = dot(of_step, terms[:, n : n + w])
        for j in range(OWN_IJ):
            label = pair[me * OWN_IJ + j]
            part = jnp.where(ab[:, n : n + w] == label, got[j * HALF : (j + 1) * HALF, :], 0.0)
            o_ref[:, j * A_ROWS + n : j * A_ROWS + n + real] = part[:, :real]


def unpack_kernel(pair, hot, sym, y_ref, o_ref):
    unpack_step(pair, hot, sym, y_ref, o_ref)


def full_unpack_kernel(pair, v_ref, y_ref, o_ref, hot, both, sym, j_ref, turn):
    @pl.when(pl.program_id(0) == 0)
    def _():
        gap = LAYERS * CAP_OUT
        unpack_tables(CAP_OUT, gap, pair, v_ref, hot, sym, j_ref, turn)
        whole = y_ref[...]
        top = whole.astype(BF)
        both[0:gap, :] = top
        both[gap : 2 * gap, :] = (whole - top.astype(F32)).astype(BF)

    unpack_step(pair, hot, sym, both, o_ref)


def table_kernel(pair, v_ref, hot, sym, j_ref, turn):
    unpack_tables(CAP_IN, CAP_LOW, pair, v_ref, hot, sym, j_ref, turn)


VM = pl.BlockSpec(memory_space=pltpu.VMEM)
SM = pl.BlockSpec(memory_space=pltpu.SMEM)


def call(kernel, args, specs, out, scratch, flops, moved, outs=VM):
    return pl.pallas_call(
        kernel,
        out_shape=out,
        in_specs=specs,
        out_specs=outs,
        scratch_shapes=scratch,
        compiler_params=pltpu.CompilerParams(vmem_limit_bytes=VMEM_LIMIT),
        cost_estimate=pl.CostEstimate(flops=flops, bytes_accessed=moved, transcendentals=0),
    )(*args)


def dense(rows, held, integrals, virt_irrep, pair_irrep):
    rows = rows.reshape(LAYERS, OWN_IJ, CDS)
    at = jnp.arange(LAYERS)
    apart = lax.axis_index("col") ^ (at & 7)
    at = (lax.axis_index("row") ^ (at >> 3)) + 2 * (apart >> 2) + 4 * (apart & 1) + 8 * (apart >> 1 & 1)
    amps = jnp.take(rows, at, axis=0).reshape(1, LAYERS * OWN_IJ, CDS)
    amps = jnp.broadcast_to(amps, (LAYERS, LAYERS * OWN_IJ, CDS))
    amps = lax.all_to_all(amps, "depth", 0, 0, tiled=True).transpose(1, 0, 2).reshape(-1, LAYERS * CDS)
    pair_sym = held[:, 0, A_ROWS + CDS : A_ROWS + 2 * CDS].reshape(-1).astype(I32)
    allowed = jnp.where(pair_irrep[:, None] == pair_sym[None, :], amps, jnp.zeros_like(amps))
    share = B_PAD // LAYERS
    padded = jnp.pad(integrals, ((0, B_PAD - B_COLS), (0, 0))).reshape(LAYERS, share, CDS * A_ROWS)
    piece = lax.all_to_all(padded, "depth", 0, 0, tiled=True).reshape(LAYERS, share, CDS, A_ROWS)
    full = jnp.einsum("jsc,sbca->jba", allowed.reshape(-1, LAYERS, CDS), piece, preferred_element_type=F32)
    back = lax.all_to_all(full, "depth", 0, 0, tiled=True).reshape(LAYERS, OWN_IJ, share, A_ROWS)
    mine = back.transpose(0, 2, 1, 3).reshape(B_PAD, OWN_IJ, A_ROWS)[:B_COLS]
    irrep_a = lax.dynamic_slice_in_dim(virt_irrep, lax.axis_index("row") * A_ROWS, A_ROWS, 0)
    irrep_b = lax.dynamic_slice_in_dim(virt_irrep, lax.axis_index("col") * B_COLS, B_COLS, 0)
    irrep_ij = lax.dynamic_slice_in_dim(pair_irrep, lax.axis_index("depth") * OWN_IJ, OWN_IJ, 0)
    ab_sym = jnp.bitwise_xor(irrep_b[:, None], irrep_a[None, :])
    mask = irrep_ij[None, :, None] == ab_sym[:, None, :]
    return jnp.where(mask, mine, jnp.float32(0.0)).reshape(B_COLS, OWN_IJ * A_ROWS)


def swap(array, axis, size, step):
    return lax.ppermute(array, axis, [(d, d ^ step) for d in range(size)])


def body(amplitudes, integrals, virt_irrep, pair_irrep, panel_c, panel_d):
    rows = LAYERS * CAP_IN
    out_rows = LAYERS * CAP_OUT
    p_row = pair_irrep[None, :]
    turn = pltpu.VMEM((8, TURN), I32)
    panel = jnp.concatenate([panel_c, panel_d])
    amps = jnp.concatenate([amplitudes, swap(amplitudes, "row", 2, 1)], axis=0)
    amps, virt_irrep, panel = lax.optimization_barrier((amps, virt_irrep, panel))
    far = swap(amps, "col", 8, 4)
    v_row = virt_irrep[None, :]
    place, notes = call(
        place_kernel,
        (virt_irrep, panel, pair_irrep, v_row, p_row),
        [SM, SM, SM, VM, VM],
        (jax.ShapeDtypeStruct((8, CDS * B_PAD), I32), jax.ShapeDtypeStruct((CAP_IN, 128), F32)),
        [pltpu.VMEM((8, B_PAD), F32), turn, pltpu.VMEM((8, 256), I32)],
        2 * 10**10,
        10**5,
        (VM, VM),
    )
    far, place, notes = lax.optimization_barrier((far, place, notes))
    amps = jnp.concatenate([amps, far], axis=0)
    amps, v_row = lax.optimization_barrier((amps, v_row))
    near = swap(amps, "col", 8, 1)
    hot, sym = call(
        table_kernel,
        (pair_irrep, v_row),
        [SM, VM],
        (
            jax.ShapeDtypeStruct((2 * OWN_IJ * HALF, rows), BF),
            jax.ShapeDtypeStruct((B_PAD, A_PAD), I32),
        ),
        [pltpu.SMEM((8,), I32), turn],
        10**9,
        10**6,
        (VM, VM),
    )
    near, hot, sym, place = lax.optimization_barrier((near, hot, sym, place))
    amps = jnp.concatenate([amps, near], axis=0)
    amps = jnp.concatenate([amps, swap(amps, "col", 8, 2)], axis=0)
    sent = call(
        pack_kernel,
        (notes, v_row, place, integrals),
        [VM] * 4,
        jax.ShapeDtypeStruct((rows, A_PAD), BF),
        [
            pltpu.VMEM((rows, CDS * B_PAD), BF),
            pltpu.VMEM((CDS * B_PAD, A_PAD), BF),
            turn,
        ],
        2 * rows * CDS * B_PAD * A_PAD,
        2 * B_COLS * CDS * A_ROWS,
    )
    last = pl.BlockSpec((rows, 128), lambda n: (0, A_PAD // 128 - 1))
    sent = pl.pallas_call(
        note_kernel,
        out_shape=jax.ShapeDtypeStruct((rows, A_PAD), BF),
        grid=(1,),
        in_specs=[
            pl.BlockSpec((CAP_IN, 128), lambda n: (0, 0)),
            pl.BlockSpec((1, 128), lambda n: (0, 0)),
            pl.BlockSpec((128, CDS), lambda n: (0, 0)),
            last,
        ],
        out_specs=last,
        scratch_shapes=[pltpu.VMEM((CAP_IN, 128), F32), pltpu.VMEM((128, CDS), F32)],
        input_output_aliases={3: 0},
        compiler_params=pltpu.CompilerParams(vmem_limit_bytes=VMEM_LIMIT),
        cost_estimate=pl.CostEstimate(flops=10**7, bytes_accessed=4 * rows * 128, transcendentals=0),
    )(notes, p_row, amps, sent)
    held = lax.all_to_all(sent.reshape(LAYERS, CAP_IN, A_PAD), "depth", 0, 0, tiled=True)
    part, terms, over = call(
        compute_kernel,
        (v_row, p_row, held.reshape(rows, A_PAD)),
        [VM] * 3,
        (
            jax.ShapeDtypeStruct((out_rows, A_PAD), F32),
            jax.ShapeDtypeStruct((rows, A_PAD), BF),
            jax.ShapeDtypeStruct((1,), I32),
        ),
        [
            pltpu.VMEM((PER * 64, 4 * CAP_IN), BF),
            pltpu.VMEM((PER * 256, A_PAD), BF),
            pltpu.VMEM((out_rows, PER * 256), BF),
            pltpu.VMEM((out_rows, 128), BF),
            turn,
            pltpu.VMEM((CAP_IN + 8, LAYERS * CDS), F32),
            pltpu.VMEM((rows, 128), F32),
            pltpu.VMEM((rows, 256), F32),
        ],
        2 * PER * 256 * A_PAD * (out_rows + 4 * CAP_IN),
        2 * rows * A_PAD,
        (VM, VM, SM),
    )

    turned = [list(range(LAYERS - 1, -1, -1))]

    def finish(kernel, array, extra, specs, scratch):
        chunks = array.reshape(LAYERS, -1, A_PAD)
        back = lax.all_to_all(chunks, "depth", 0, 0, tiled=True, axis_index_groups=turned)
        return pl.pallas_call(
            kernel,
            out_shape=jax.ShapeDtypeStruct((B_COLS, OWN_IJ * A_ROWS), F32),
            grid=(2,),
            in_specs=[SM, *specs, whole(array.shape)],
            out_specs=pl.BlockSpec((HALF, OWN_IJ * A_ROWS), lambda t: (t, 0)),
            scratch_shapes=scratch,
            compiler_params=pltpu.CompilerParams(vmem_limit_bytes=VMEM_LIMIT),
            cost_estimate=pl.CostEstimate(
                flops=4 * OWN_IJ * HALF * rows * A_PAD,
                bytes_accessed=4 * B_COLS * OWN_IJ * A_ROWS,
                transcendentals=0,
            ),
        )(pair_irrep, *extra, back.reshape(array.shape))

    def whole(shape):
        return pl.BlockSpec(shape, lambda t: (0, 0))

    def usual(part, terms, held, amps, hot, sym):
        return finish(unpack_kernel, terms, (hot, sym), [whole(hot.shape), whole(sym.shape)], [])

    def fuller(part, terms, held, amps, hot, sym):
        scratch = [
            pltpu.VMEM((2 * OWN_IJ * HALF, 2 * out_rows), BF),
            pltpu.VMEM((2 * out_rows, A_PAD), BF),
            pltpu.VMEM((B_PAD, A_PAD), I32),
            pltpu.SMEM((8,), I32),
            turn,
        ]
        return finish(full_unpack_kernel, part, (v_row,), [whole((1, NV))], scratch)

    def general(part, terms, held, amps, hot, sym):
        return dense(amps, held, integrals, virt_irrep, pair_irrep)

    return lax.switch(over[0], (usual, fuller, general), part, terms, held, amps, hot, sym)


def solution(mesh):
    return jax.shard_map(
        body,
        mesh=mesh,
        in_specs=(
            P(("row", "col"), "depth"),
            P("col", ("row", "depth")),
            P(),
            P(),
            P("depth"),
            P("depth"),
        ),
        out_specs=P("col", ("row", "depth")),
        check_vma=False,
    )
```

```python
import jax
import jax.numpy as jnp
from jax import lax
from jax.experimental import pallas as pl
from jax.experimental.pallas import tpu as pltpu
from jax.sharding import PartitionSpec as P

NV = 1200
LAYERS = 16
A_ROWS = 600
B_COLS = 150
A_PAD = 640
B_PAD = 160
CDS = 16
OWN_IJ = 8
CAP_IN = 40
CAP_OUT = 24
CAP_LOW = 20
HALF = 80
PER = 10
TURN = 1280
META = A_ROWS - 512
BF = jnp.bfloat16
F32 = jnp.float32
I32 = jnp.int32
VMEM_LIMIT = 20 * 1024 * 1024
DN = (((1,), (0,)), ((), ()))


def iota(shape, dim):
    return lax.broadcasted_iota(I32, shape, dim)


def dot(x, y):
    return lax.dot_general(x, y, DN, preferred_element_type=F32)


def to_col(row):
    size = row.shape[1]
    eye = iota((size, size), 0) == iota((size, size), 1)
    spread = jnp.where(eye, jnp.broadcast_to(row.astype(F32), (size, size)), 0.0)
    return jnp.sum(spread, axis=1, keepdims=True).astype(I32)


def ones(mask):
    return jnp.where(mask, 1.0, 0.0)


def ranks(b_row):
    key_row = b_row * 256 + iota(b_row.shape, 1)
    key_col = to_col(key_row)
    rank_row = jnp.sum(ones(key_col < key_row), axis=0, keepdims=True).astype(I32)
    rank_col = jnp.sum(ones(key_row < key_col), axis=1, keepdims=True).astype(I32)
    return rank_row, rank_col, jnp.right_shift(key_col, 8)


def irreps(v_ref):
    whole = jnp.broadcast_to(v_ref[...], (8, TURN))
    a_at = lax.axis_index("row") * A_ROWS
    b_at = lax.axis_index("col") * B_COLS
    a_row = pltpu.roll(whole, TURN - a_at, 1)[0:1, 0:A_PAD]
    b_row = pltpu.roll(whole, TURN - b_at, 1)[0:1, 0:B_PAD]
    a_row = jnp.where(iota((1, A_PAD), 1) < A_ROWS, a_row, 64)
    return a_row, jnp.where(iota((1, B_PAD), 1) < B_COLS, b_row, 16)


def own_irreps(b_row):
    me = lax.axis_index("depth")
    rank_row, _, _ = ranks(b_row)
    beta = []
    for i in range(PER):
        mine = rank_row == i * LAYERS + me
        beta.append(jnp.sum(jnp.where(mine, b_row, 0).astype(F32), axis=1, keepdims=True).astype(I32))
    return beta


def class_counts(labels):
    count = [sum((label == y).astype(I32) for label in labels) for y in range(8)]
    order = [sum([(labels[k] == labels[j]).astype(I32) for k in range(j)], jnp.int32(0)) for j in range(len(labels))]
    return count, order


def slots(pair_ref):
    p_row = pair_ref[...]
    p_col = to_col(p_row)
    square = (128, 128)
    alike = p_row == p_col
    row = jnp.sum(ones(jnp.logical_and(alike, iota(square, 0) < iota(square, 1))), axis=0, keepdims=True)
    col = jnp.sum(ones(jnp.logical_and(alike, iota(square, 1) < iota(square, 0))), axis=1, keepdims=True)
    return row.astype(I32), col.astype(I32), p_col


def place_kernel(labels, pair, v_ref, pair_ref, q_ref, m_ref, s_ref, each):
    me = lax.axis_index("depth")
    _, b_row = irreps(v_ref)
    g = [labels[0, labels[0, NV + j]] ^ labels[0, labels[0, NV + CDS + j]] for j in range(CDS)]
    rank_row, rank_col, b_col = ranks(b_row)
    same = jnp.logical_and((rank_row & 15) == (rank_col & 15), rank_col < rank_row)
    diff = b_col ^ b_row
    before = [jnp.sum(ones(jnp.logical_and(same, diff == y)), axis=0, keepdims=True) for y in range(8)]
    count, order = class_counts(g)
    count = [c.astype(F32) for c in count]
    for x in range(8):
        s_ref[x : x + 1, :] = sum(count[y ^ x] * before[y] for y in range(8))
    first = (rank_row & 15) * CAP_IN
    for j in range(CDS):
        place = s_ref[pl.ds(g[j], 1), :] + order[j].astype(F32)
        q_ref[0:1, j * B_PAD : (j + 1) * B_PAD] = first + place.astype(I32)

    own = [pair[me * OWN_IJ + j] for j in range(OWN_IJ)]
    for c in range(8):
        each[c : c + 1, 0:B_COLS] = v_ref[0:1, c * B_COLS : (c + 1) * B_COLS]
    of_col = each[:, 0:B_COLS]
    chunk = jnp.maximum(15 - iota((8, 128), 1), 0)
    start = jnp.zeros((8, 1), I32)
    dealt = []
    for h in range(8):
        end = start + jnp.sum(ones(of_col == h), axis=1, keepdims=True).astype(I32)
        dealt.append((jnp.right_shift(end + chunk, 4) - jnp.right_shift(start + chunk, 4)).astype(F32))
        start = end
    over = jnp.zeros((8, 128), F32)
    results = [c.astype(F32) for c in class_counts(own)[0]]
    for x in range(8):
        stacked = sum(count[y ^ x] * dealt[y] for y in range(8))
        back = sum(results[y ^ x] * dealt[y] for y in range(8))
        wrong = jnp.logical_or(stacked > CAP_IN, back > CAP_OUT)
        over = jnp.maximum(over, jnp.where(wrong, 2.0, ones(back > CAP_LOW)))
    slot_row, _, _ = slots(pair_ref)
    crowd = jnp.max(slot_row, axis=1, keepdims=True) >= CAP_IN
    over = jnp.maximum(jnp.max(over, axis=(0, 1), keepdims=True), jnp.where(crowd, 2.0, 0.0))
    lane = iota((1, CDS), 1)
    m_ref[...] = jnp.zeros_like(m_ref)
    m_ref[0:1, META + CDS : META + 2 * CDS] = sum(jnp.where(lane == j, g[j], 0) for j in range(CDS)).astype(F32)
    m_ref[1:2, META + CDS : META + 2 * CDS] = jnp.broadcast_to(over, (1, CDS))


def pack_kernel(g_ref, v_ref, q_ref, eri_ref, x_ref, hot, masked):
    a_row, b_row = irreps(v_ref)
    b_col = to_col(b_row)
    rows = LAYERS * CAP_IN
    for t in range(CDS * B_PAD // 512):
        at = slice(t * 512, (t + 1) * 512)
        hot[:, at] = ones(iota((rows, 512), 0) == q_ref[0:1, at]).astype(BF)
    masked[:, 512:A_PAD] = jnp.zeros((CDS * B_PAD, 128), BF)
    for j in range(CDS):
        masked[(j + 1) * B_PAD - 16 : (j + 1) * B_PAD, 0:512] = jnp.zeros((16, 512), BF)
    ab = (b_col ^ a_row)[:B_COLS, :A_ROWS].astype(F32).astype(BF)
    for j in range(CDS):
        slab = eri_ref[:, j * A_ROWS : (j + 1) * A_ROWS]
        label = g_ref[0:1, META + CDS + j : META + CDS + j + 1].astype(BF)
        masked[j * B_PAD : j * B_PAD + B_COLS, 0:A_ROWS] = jnp.where(ab == label, slab, jnp.zeros_like(slab))
    for n, w in ((0, 256), (256, 256), (512, 128)):
        x_ref[:, n : n + w] = dot(hot[...], masked[:, n : n + w]).astype(BF)


def note_kernel(g_ref, pair_ref, amp_ref, x_in, x_ref, m_ref, amps):
    slot_row, _, p_col = slots(pair_ref)
    g_row = g_ref[0:1, META + CDS : META + 2 * CDS].astype(I32)
    for k in range(16):
        apart = (k >> 1 & 1) * 4 + (k >> 2 & 1) + (k >> 3) * 2
        block = (lax.axis_index("row") ^ (k & 1)) * 8 + (lax.axis_index("col") ^ apart)
        amps[pl.ds(pl.multiple_of(block * 8, 8), 8), :] = amp_ref[k * 8 : (k + 1) * 8, :].astype(F32)
    allowed = jnp.where(p_col == g_row, amps[...], 0.0).astype(BF)
    in_slot = ones(iota((CAP_IN, 128), 0) == slot_row).astype(BF)
    m_ref[...] = g_ref[...]
    m_ref[:, META : META + CDS] = dot(in_slot, allowed)
    note = m_ref[...]
    whole = jnp.concatenate([note] * LAYERS, axis=0)
    x_ref[...] = (x_in[...].astype(F32) + whole).astype(BF)


def compute_kernel(v_ref, pair_ref, y_ref, x_ref, pair_out, over_ref, hot, eri, amp, hot2, notes, tail, stage):
    me = lax.axis_index("depth")
    tail[...] = y_ref[:, A_PAD - 128 : A_PAD].astype(F32)
    for c in range(LAYERS):
        at = slice(c * CDS, (c + 1) * CDS)
        notes[0:CAP_IN, at] = tail[c * CAP_IN : (c + 1) * CAP_IN, META : META + CDS]
        notes[CAP_IN : CAP_IN + 8, at] = tail[c * CAP_IN : c * CAP_IN + 8, META + CDS : META + 2 * CDS]
    over_ref[0] = jnp.max(notes[CAP_IN + 1 : CAP_IN + 2, :]).astype(I32)
    a_row, b_row = irreps(v_ref)
    beta = own_irreps(b_row)

    g_row = notes[CAP_IN : CAP_IN + 1, :].astype(I32)
    g_col = to_col(g_row)
    wide = (256, 256)
    same = jnp.right_shift(iota(wide, 0), 4) == jnp.right_shift(iota(wide, 1), 4)
    earlier = jnp.logical_and(same, iota(wide, 1) < iota(wide, 0))
    order = jnp.sum(ones(jnp.logical_and(earlier, g_row == g_col)), axis=1, keepdims=True)
    lane = iota((1, 128), 1)
    part, label = jnp.right_shift(lane, 3), lane & 7
    own = sum(jnp.where(part == i, beta[i], 0) for i in range(PER))
    wanted = (label ^ own) ^ g_col
    seen = sum(ones(jnp.logical_and(part > i, wanted == beta[i])) for i in range(PER - 1))
    count = dot(ones(same).astype(BF), ones(g_col == label).astype(BF))
    square = (128, 128)
    by_part = ones(jnp.right_shift(iota(square, 0), 3) == iota(square, 1)).astype(BF)
    place = dot((seen * count).astype(BF), by_part) + order
    rows = iota((256, 1), 0)
    place = place.astype(I32) + (jnp.right_shift(rows, 4) & 3) * CAP_IN

    four = 4 * CAP_IN
    sym = [a_row ^ beta[i] for i in range(PER)]
    for k in range(4):
        at = slice(k * 64, (k + 1) * 64)
        for i in range(PER):
            hot[i * 64 : (i + 1) * 64, :] = ones(iota((64, four), 1) == place[at, i : i + 1]).astype(BF)
        for n, w in ((0, 256), (256, 256), (512, 128)):
            got = dot(hot[...], y_ref[k * four : (k + 1) * four, n : n + w])
            for i in range(PER):
                keep = sym[i][:, n : n + w] == g_col[at, :]
                eri[i * 256 + k * 64 : i * 256 + (k + 1) * 64, n : n + w] = jnp.where(
                    keep, got[i * 64 : (i + 1) * 64, :], 0.0
                ).astype(BF)

    _, slot_col, p_col = slots(pair_ref)
    from_slot = ones(iota((128, CAP_IN), 1) == slot_col).astype(BF)
    allowed = jnp.where(p_col == g_row, dot(from_slot, notes[0:CAP_IN, :].astype(BF)), 0.0).astype(BF)
    p_row = pair_ref[...]
    same2 = jnp.right_shift(iota(square, 0), 3) == jnp.right_shift(iota(square, 1), 3)
    earlier2 = jnp.logical_and(same2, iota(square, 0) < iota(square, 1))
    order2 = jnp.sum(ones(jnp.logical_and(earlier2, p_row == p_col)), axis=0, keepdims=True)
    row = iota((128, 1), 0)
    part2, label2 = jnp.right_shift(row, 3), row & 7
    own2 = sum(jnp.where(part2 == i, beta[i], 0) for i in range(PER))
    wanted2 = (label2 ^ own2) ^ p_row
    seen2 = sum(ones(jnp.logical_and(part2 > i, wanted2 == beta[i])) for i in range(PER - 1))
    count2 = dot(ones(label2 == p_row).astype(BF), ones(same2).astype(BF))
    short = (16, 128)
    by_part2 = ones(jnp.right_shift(iota(short, 1), 3) == iota(short, 0)).astype(BF)
    place2 = dot(by_part2, (seen2 * count2).astype(BF)) + order2
    place2 = place2.astype(I32) + (LAYERS - 1 - jnp.right_shift(iota((1, 128), 1), 3)) * CAP_OUT
    out_rows = LAYERS * CAP_OUT
    for i in range(PER):
        hot2[...] = ones(iota((out_rows, 128), 0) == place2[i : i + 1, :]).astype(BF)
        amp[:, i * 256 : (i + 1) * 256] = dot(hot2[...], allowed).astype(BF)
    for n, w in ((0, 256), (256, 256), (512, 128)):
        got = dot(amp[...], eri[:, n : n + w])
        x_ref[:, n : n + w] = got
        high = got.astype(BF).astype(F32)
        low = got - high
        for k in range(LAYERS):
            at = slice(k * CAP_OUT, k * CAP_OUT + CAP_LOW)
            stage[k * CAP_IN : k * CAP_IN + CAP_LOW, 0:w] = high[at, :]
            stage[k * CAP_IN + CAP_LOW : (k + 1) * CAP_IN, 0:w] = low[at, :]
        pair_out[:, n : n + w] = stage[:, 0:w].astype(BF)


def unpack_tables(stride, gap, pair, v_ref, hot, sym, j_ref):
    me = lax.axis_index("depth")
    labels = [pair[me * OWN_IJ + j] for j in range(OWN_IJ)]
    width = hot.shape[1]
    a_row, b_row = irreps(v_ref)
    count, order = class_counts(labels)
    for y in range(8):
        j_ref[y] = count[y]
    rank_row, rank_col, b_col = ranks(b_row)
    same = jnp.logical_and((rank_row & 15) == (rank_col & 15), rank_row < rank_col)
    diff = b_col ^ b_row
    before = [jnp.sum(ones(jnp.logical_and(same, diff == y)), axis=1, keepdims=True) for y in range(8)]
    first = (LAYERS - 1 - (rank_col & 15)) * stride
    for j in range(OWN_IJ):
        place = sum(j_ref[y ^ labels[j]].astype(F32) * before[y] for y in range(8)) + order[j].astype(F32)
        place = first + place.astype(I32)
        for t in range(2):
            mine = place[t * HALF : (t + 1) * HALF, :]
            lane = iota((HALF, width), 1)
            at = (t * OWN_IJ + j) * HALF
            hot[at : at + HALF, :] = ones(jnp.logical_or(lane == mine, lane == mine + gap)).astype(BF)
    sym[...] = b_col ^ a_row


def unpack_step(pair, hot, sym, terms, o_ref):
    step = pl.program_id(0)
    me = lax.axis_index("depth")
    rows = OWN_IJ * HALF
    of_step = hot[pl.ds(pl.multiple_of(step * rows, rows), rows), :]
    ab = sym[pl.ds(pl.multiple_of(step * HALF, HALF), HALF), :]
    for n, w, real in ((0, 256, 256), (256, 256, 256), (512, 128, A_ROWS - 512)):
        got = dot(of_step, terms[:, n : n + w])
        for j in range(OWN_IJ):
            label = pair[me * OWN_IJ + j]
            part = jnp.where(ab[:, n : n + w] == label, got[j * HALF : (j + 1) * HALF, :], 0.0)
            o_ref[:, j * A_ROWS + n : j * A_ROWS + n + real] = part[:, :real]


def unpack_kernel(pair, hot, sym, y_ref, o_ref):
    unpack_step(pair, hot, sym, y_ref, o_ref)


def full_unpack_kernel(pair, v_ref, y_ref, o_ref, hot, both, sym, j_ref):
    @pl.when(pl.program_id(0) == 0)
    def _():
        gap = LAYERS * CAP_OUT
        unpack_tables(CAP_OUT, gap, pair, v_ref, hot, sym, j_ref)
        whole = y_ref[...]
        top = whole.astype(BF)
        both[0:gap, :] = top
        both[gap : 2 * gap, :] = (whole - top.astype(F32)).astype(BF)

    unpack_step(pair, hot, sym, both, o_ref)


def table_kernel(pair, v_ref, hot, sym, j_ref):
    unpack_tables(CAP_IN, CAP_LOW, pair, v_ref, hot, sym, j_ref)


VM = pl.BlockSpec(memory_space=pltpu.VMEM)
SM = pl.BlockSpec(memory_space=pltpu.SMEM)


def call(kernel, args, specs, out, scratch, flops, moved, outs=VM):
    return pl.pallas_call(
        kernel,
        out_shape=out,
        in_specs=specs,
        out_specs=outs,
        scratch_shapes=scratch,
        compiler_params=pltpu.CompilerParams(vmem_limit_bytes=VMEM_LIMIT),
        cost_estimate=pl.CostEstimate(flops=flops, bytes_accessed=moved, transcendentals=0),
    )(*args)


def dense(rows, held, integrals, virt_irrep, pair_irrep):
    rows = rows.reshape(LAYERS, OWN_IJ, CDS)
    at = jnp.arange(LAYERS)
    apart = lax.axis_index("col") ^ (at & 7)
    at = (lax.axis_index("row") ^ (at >> 3)) + 2 * (apart >> 2) + 4 * (apart & 1) + 8 * (apart >> 1 & 1)
    amps = jnp.take(rows, at, axis=0).reshape(1, LAYERS * OWN_IJ, CDS)
    amps = jnp.broadcast_to(amps, (LAYERS, LAYERS * OWN_IJ, CDS))
    amps = lax.all_to_all(amps, "depth", 0, 0, tiled=True).transpose(1, 0, 2).reshape(-1, LAYERS * CDS)
    pair_sym = held[:, 0, A_ROWS + CDS : A_ROWS + 2 * CDS].reshape(-1).astype(I32)
    allowed = jnp.where(pair_irrep[:, None] == pair_sym[None, :], amps, jnp.zeros_like(amps))
    share = B_PAD // LAYERS
    padded = jnp.pad(integrals, ((0, B_PAD - B_COLS), (0, 0))).reshape(LAYERS, share, CDS * A_ROWS)
    piece = lax.all_to_all(padded, "depth", 0, 0, tiled=True).reshape(LAYERS, share, CDS, A_ROWS)
    full = jnp.einsum("jsc,sbca->jba", allowed.reshape(-1, LAYERS, CDS), piece, preferred_element_type=F32)
    back = lax.all_to_all(full, "depth", 0, 0, tiled=True).reshape(LAYERS, OWN_IJ, share, A_ROWS)
    mine = back.transpose(0, 2, 1, 3).reshape(B_PAD, OWN_IJ, A_ROWS)[:B_COLS]
    irrep_a = lax.dynamic_slice_in_dim(virt_irrep, lax.axis_index("row") * A_ROWS, A_ROWS, 0)
    irrep_b = lax.dynamic_slice_in_dim(virt_irrep, lax.axis_index("col") * B_COLS, B_COLS, 0)
    irrep_ij = lax.dynamic_slice_in_dim(pair_irrep, lax.axis_index("depth") * OWN_IJ, OWN_IJ, 0)
    ab_sym = jnp.bitwise_xor(irrep_b[:, None], irrep_a[None, :])
    mask = irrep_ij[None, :, None] == ab_sym[:, None, :]
    return jnp.where(mask, mine, jnp.float32(0.0)).reshape(B_COLS, OWN_IJ * A_ROWS)


def swap(array, axis, size, step):
    return lax.ppermute(array, axis, [(d, d ^ step) for d in range(size)])


def body(amplitudes, integrals, virt_irrep, pair_irrep, panel_c, panel_d):
    rows = LAYERS * CAP_IN
    out_rows = LAYERS * CAP_OUT
    p_row = pair_irrep[None, :]
    v_row = jnp.concatenate([virt_irrep, panel_c, panel_d, jnp.zeros(TURN - NV - 2 * CDS, I32)])[None, :]
    amps = jnp.concatenate([amplitudes, swap(amplitudes, "row", 2, 1)], axis=0)
    amps, v_row = lax.optimization_barrier((amps, v_row))
    far = swap(amps, "col", 8, 4)
    place, notes = call(
        place_kernel,
        (v_row, pair_irrep, v_row, p_row),
        [SM, SM, VM, VM],
        (jax.ShapeDtypeStruct((8, CDS * B_PAD), I32), jax.ShapeDtypeStruct((CAP_IN, 128), F32)),
        [pltpu.VMEM((8, B_PAD), F32), pltpu.VMEM((8, 256), I32)],
        2 * 10**10,
        10**5,
        (VM, VM),
    )
    far, place, notes = lax.optimization_barrier((far, place, notes))
    amps = jnp.concatenate([amps, far], axis=0)
    amps, v_row = lax.optimization_barrier((amps, v_row))
    near = swap(amps, "col", 8, 1)
    hot, sym = call(
        table_kernel,
        (pair_irrep, v_row),
        [SM, VM],
        (
            jax.ShapeDtypeStruct((2 * OWN_IJ * HALF, rows), BF),
            jax.ShapeDtypeStruct((B_PAD, A_PAD), I32),
        ),
        [pltpu.SMEM((8,), I32)],
        10**9,
        10**6,
        (VM, VM),
    )
    near, hot, sym, place = lax.optimization_barrier((near, hot, sym, place))
    amps = jnp.concatenate([amps, near], axis=0)
    amps = jnp.concatenate([amps, swap(amps, "col", 8, 2)], axis=0)
    sent = call(
        pack_kernel,
        (notes, v_row, place, integrals),
        [VM] * 4,
        jax.ShapeDtypeStruct((rows, A_PAD), BF),
        [
            pltpu.VMEM((rows, CDS * B_PAD), BF),
            pltpu.VMEM((CDS * B_PAD, A_PAD), BF),
        ],
        2 * rows * CDS * B_PAD * A_PAD,
        2 * B_COLS * CDS * A_ROWS,
    )
    last = pl.BlockSpec((rows, 128), lambda n: (0, A_PAD // 128 - 1))
    sent = pl.pallas_call(
        note_kernel,
        out_shape=jax.ShapeDtypeStruct((rows, A_PAD), BF),
        grid=(1,),
        in_specs=[
            pl.BlockSpec((CAP_IN, 128), lambda n: (0, 0)),
            pl.BlockSpec((1, 128), lambda n: (0, 0)),
            pl.BlockSpec((128, CDS), lambda n: (0, 0)),
            last,
        ],
        out_specs=last,
        scratch_shapes=[pltpu.VMEM((CAP_IN, 128), F32), pltpu.VMEM((128, CDS), F32)],
        input_output_aliases={3: 0},
        compiler_params=pltpu.CompilerParams(vmem_limit_bytes=VMEM_LIMIT),
        cost_estimate=pl.CostEstimate(flops=10**7, bytes_accessed=4 * rows * 128, transcendentals=0),
    )(notes, p_row, amps, sent)
    held = lax.all_to_all(sent.reshape(LAYERS, CAP_IN, A_PAD), "depth", 0, 0, tiled=True)
    part, terms, over = call(
        compute_kernel,
        (v_row, p_row, held.reshape(rows, A_PAD)),
        [VM] * 3,
        (
            jax.ShapeDtypeStruct((out_rows, A_PAD), F32),
            jax.ShapeDtypeStruct((rows, A_PAD), BF),
            jax.ShapeDtypeStruct((1,), I32),
        ),
        [
            pltpu.VMEM((PER * 64, 4 * CAP_IN), BF),
            pltpu.VMEM((PER * 256, A_PAD), BF),
            pltpu.VMEM((out_rows, PER * 256), BF),
            pltpu.VMEM((out_rows, 128), BF),
            pltpu.VMEM((CAP_IN + 8, LAYERS * CDS), F32),
            pltpu.VMEM((rows, 128), F32),
            pltpu.VMEM((rows, 256), F32),
        ],
        2 * PER * 256 * A_PAD * (out_rows + 4 * CAP_IN),
        2 * rows * A_PAD,
        (VM, VM, SM),
    )

    turned = [list(range(LAYERS - 1, -1, -1))]

    def finish(kernel, array, extra, specs, scratch):
        chunks = array.reshape(LAYERS, -1, A_PAD)
        back = lax.all_to_all(chunks, "depth", 0, 0, tiled=True, axis_index_groups=turned)
        return pl.pallas_call(
            kernel,
            out_shape=jax.ShapeDtypeStruct((B_COLS, OWN_IJ * A_ROWS), F32),
            grid=(2,),
            in_specs=[SM, *specs, whole(array.shape)],
            out_specs=pl.BlockSpec((HALF, OWN_IJ * A_ROWS), lambda t: (t, 0)),
            scratch_shapes=scratch,
            compiler_params=pltpu.CompilerParams(vmem_limit_bytes=VMEM_LIMIT),
            cost_estimate=pl.CostEstimate(
                flops=4 * OWN_IJ * HALF * rows * A_PAD,
                bytes_accessed=4 * B_COLS * OWN_IJ * A_ROWS,
                transcendentals=0,
            ),
        )(pair_irrep, *extra, back.reshape(array.shape))

    def whole(shape):
        return pl.BlockSpec(shape, lambda t: (0, 0))

    def usual(part, terms, held, amps, hot, sym):
        return finish(unpack_kernel, terms, (hot, sym), [whole(hot.shape), whole(sym.shape)], [])

    def fuller(part, terms, held, amps, hot, sym):
        scratch = [
            pltpu.VMEM((2 * OWN_IJ * HALF, 2 * out_rows), BF),
            pltpu.VMEM((2 * out_rows, A_PAD), BF),
            pltpu.VMEM((B_PAD, A_PAD), I32),
            pltpu.SMEM((8,), I32),
        ]
        return finish(full_unpack_kernel, part, (v_row,), [whole((1, TURN))], scratch)

    def general(part, terms, held, amps, hot, sym):
        return dense(amps, held, integrals, virt_irrep, pair_irrep)

    return lax.switch(over[0], (usual, fuller, general), part, terms, held, amps, hot, sym)


def solution(mesh):
    return jax.shard_map(
        body,
        mesh=mesh,
        in_specs=(
            P(("row", "col"), "depth"),
            P("col", ("row", "depth")),
            P(),
            P(),
            P("depth"),
            P("depth"),
        ),
        out_specs=P("col", ("row", "depth")),
        check_vma=False,
    )
```

```python
import jax
import jax.numpy as jnp
from jax import lax
from jax.experimental import pallas as pl
from jax.experimental.pallas import tpu as pltpu
from jax.sharding import PartitionSpec as P

NV = 1200
LAYERS = 16
A_ROWS = 600
B_COLS = 150
A_PAD = 640
B_PAD = 160
CDS = 16
OWN_IJ = 8
CAP_IN = 40
CAP_OUT = 24
CAP_LOW = 20
HALF = 80
PER = 10
TURN = 1280
META = A_ROWS - 512
BF = jnp.bfloat16
F32 = jnp.float32
I32 = jnp.int32
VMEM_LIMIT = 20 * 1024 * 1024
DN = (((1,), (0,)), ((), ()))


def iota(shape, dim):
    return lax.broadcasted_iota(I32, shape, dim)


def dot(x, y):
    return lax.dot_general(x, y, DN, preferred_element_type=F32)


def to_col(row):
    size = row.shape[1]
    eye = iota((size, size), 0) == iota((size, size), 1)
    spread = jnp.where(eye, jnp.broadcast_to(row.astype(F32), (size, size)), 0.0)
    return jnp.sum(spread, axis=1, keepdims=True).astype(I32)


def ones(mask):
    return jnp.where(mask, 1.0, 0.0)


def ranks(b_row):
    key_row = b_row * 256 + iota(b_row.shape, 1)
    key_col = to_col(key_row)
    rank_row = jnp.sum(ones(key_col < key_row), axis=0, keepdims=True).astype(I32)
    rank_col = jnp.sum(ones(key_row < key_col), axis=1, keepdims=True).astype(I32)
    return rank_row, rank_col, jnp.right_shift(key_col, 8)


def irreps(v_ref):
    whole = jnp.broadcast_to(v_ref[...], (8, TURN))
    a_at = lax.axis_index("row") * A_ROWS
    b_at = lax.axis_index("col") * B_COLS
    a_row = pltpu.roll(whole, TURN - a_at, 1)[0:1, 0:A_PAD]
    b_row = pltpu.roll(whole, TURN - b_at, 1)[0:1, 0:B_PAD]
    a_row = jnp.where(iota((1, A_PAD), 1) < A_ROWS, a_row, 64)
    return a_row, jnp.where(iota((1, B_PAD), 1) < B_COLS, b_row, 16)


def own_irreps(b_row):
    me = lax.axis_index("depth")
    rank_row, _, _ = ranks(b_row)
    beta = []
    for i in range(PER):
        mine = rank_row == i * LAYERS + me
        beta.append(jnp.sum(jnp.where(mine, b_row, 0).astype(F32), axis=1, keepdims=True).astype(I32))
    return beta


def class_counts(labels):
    count = [sum((label == y).astype(I32) for label in labels) for y in range(8)]
    order = [sum([(labels[k] == labels[j]).astype(I32) for k in range(j)], jnp.int32(0)) for j in range(len(labels))]
    return count, order


def slots(pair_ref):
    p_row = pair_ref[...]
    p_col = to_col(p_row)
    square = (128, 128)
    alike = p_row == p_col
    row = jnp.sum(ones(jnp.logical_and(alike, iota(square, 0) < iota(square, 1))), axis=0, keepdims=True)
    col = jnp.sum(ones(jnp.logical_and(alike, iota(square, 1) < iota(square, 0))), axis=1, keepdims=True)
    return row.astype(I32), col.astype(I32), p_col


def place_kernel(labels, pair, v_ref, pair_ref, q_ref, m_ref, s_ref, each):
    me = lax.axis_index("depth")
    _, b_row = irreps(v_ref)
    g = [labels[0, labels[0, NV + j]] ^ labels[0, labels[0, NV + CDS + j]] for j in range(CDS)]
    rank_row, rank_col, b_col = ranks(b_row)
    same = jnp.logical_and((rank_row & 15) == (rank_col & 15), rank_col < rank_row)
    diff = b_col ^ b_row
    before = [jnp.sum(ones(jnp.logical_and(same, diff == y)), axis=0, keepdims=True) for y in range(8)]
    count, order = class_counts(g)
    count = [c.astype(F32) for c in count]
    for x in range(8):
        s_ref[x : x + 1, :] = sum(count[y ^ x] * before[y] for y in range(8))
    first = (rank_row & 15) * CAP_IN
    for j in range(CDS):
        place = s_ref[pl.ds(g[j], 1), :] + order[j].astype(F32)
        q_ref[0:1, j * B_PAD : (j + 1) * B_PAD] = first + place.astype(I32)

    own = [pair[me * OWN_IJ + j] for j in range(OWN_IJ)]
    for c in range(8):
        each[c : c + 1, 0:B_COLS] = v_ref[0:1, c * B_COLS : (c + 1) * B_COLS]
    of_col = each[:, 0:B_COLS]
    chunk = jnp.maximum(15 - iota((8, 128), 1), 0)
    start = jnp.zeros((8, 1), I32)
    dealt = []
    for h in range(8):
        end = start + jnp.sum(ones(of_col == h), axis=1, keepdims=True).astype(I32)
        dealt.append((jnp.right_shift(end + chunk, 4) - jnp.right_shift(start + chunk, 4)).astype(F32))
        start = end
    over = jnp.zeros((8, 128), F32)
    results = [c.astype(F32) for c in class_counts(own)[0]]
    for x in range(8):
        stacked = sum(count[y ^ x] * dealt[y] for y in range(8))
        back = sum(results[y ^ x] * dealt[y] for y in range(8))
        wrong = jnp.logical_or(stacked > CAP_IN, back > CAP_OUT)
        over = jnp.maximum(over, jnp.where(wrong, 2.0, ones(back > CAP_LOW)))
    slot_row, _, _ = slots(pair_ref)
    crowd = jnp.max(slot_row, axis=1, keepdims=True) >= CAP_IN
    over = jnp.maximum(jnp.max(over, axis=(0, 1), keepdims=True), jnp.where(crowd, 2.0, 0.0))
    lane = iota((1, CDS), 1)
    m_ref[...] = jnp.zeros_like(m_ref)
    m_ref[0:1, META + CDS : META + 2 * CDS] = sum(jnp.where(lane == j, g[j], 0) for j in range(CDS)).astype(F32)
    m_ref[1:2, META + CDS : META + 2 * CDS] = jnp.broadcast_to(over, (1, CDS))


def pack_kernel(g_ref, v_ref, q_ref, eri_ref, x_ref, hot, masked):
    a_row, b_row = irreps(v_ref)
    b_col = to_col(b_row)
    rows = LAYERS * CAP_IN
    for t in range(CDS * B_PAD // 512):
        at = slice(t * 512, (t + 1) * 512)
        hot[:, at] = ones(iota((rows, 512), 0) == q_ref[0:1, at]).astype(BF)
    masked[:, 512:A_PAD] = jnp.zeros((CDS * B_PAD, 128), BF)
    for j in range(CDS):
        masked[(j + 1) * B_PAD - 16 : (j + 1) * B_PAD, 0:512] = jnp.zeros((16, 512), BF)
    ab = (b_col ^ a_row)[:B_COLS, :A_ROWS].astype(F32).astype(BF)
    for j in range(CDS):
        slab = eri_ref[:, j * A_ROWS : (j + 1) * A_ROWS]
        label = g_ref[0:1, META + CDS + j : META + CDS + j + 1].astype(BF)
        masked[j * B_PAD : j * B_PAD + B_COLS, 0:A_ROWS] = jnp.where(ab == label, slab, jnp.zeros_like(slab))
    for n, w in ((0, 256), (256, 256), (512, 128)):
        x_ref[:, n : n + w] = dot(hot[...], masked[:, n : n + w]).astype(BF)


def note_kernel(g_ref, pair_ref, amp_ref, x_in, x_ref, m_ref, amps):
    slot_row, _, p_col = slots(pair_ref)
    g_row = g_ref[0:1, META + CDS : META + 2 * CDS].astype(I32)
    for k in range(16):
        apart = (k >> 1 & 1) * 4 + (k >> 2 & 1) + (k >> 3) * 2
        block = (lax.axis_index("row") ^ (k & 1)) * 8 + (lax.axis_index("col") ^ apart)
        amps[pl.ds(pl.multiple_of(block * 8, 8), 8), :] = amp_ref[k * 8 : (k + 1) * 8, :].astype(F32)
    allowed = jnp.where(p_col == g_row, amps[...], 0.0).astype(BF)
    in_slot = ones(iota((CAP_IN, 128), 0) == slot_row).astype(BF)
    m_ref[...] = g_ref[...]
    m_ref[:, META : META + CDS] = dot(in_slot, allowed)
    note = m_ref[...]
    whole = jnp.concatenate([note] * LAYERS, axis=0)
    x_ref[...] = (x_in[...].astype(F32) + whole).astype(BF)


def compute_kernel(v_ref, pair_ref, y_ref, x_ref, pair_out, over_ref, hot, eri, amp, hot2, notes, tail, stage):
    me = lax.axis_index("depth")
    tail[...] = y_ref[:, A_PAD - 128 : A_PAD].astype(F32)
    for c in range(LAYERS):
        at = slice(c * CDS, (c + 1) * CDS)
        notes[0:CAP_IN, at] = tail[c * CAP_IN : (c + 1) * CAP_IN, META : META + CDS]
        notes[CAP_IN : CAP_IN + 8, at] = tail[c * CAP_IN : c * CAP_IN + 8, META + CDS : META + 2 * CDS]
    over_ref[0] = jnp.max(notes[CAP_IN + 1 : CAP_IN + 2, :]).astype(I32)
    a_row, b_row = irreps(v_ref)
    beta = own_irreps(b_row)

    g_row = notes[CAP_IN : CAP_IN + 1, :].astype(I32)
    g_col = to_col(g_row)
    wide = (256, 256)
    same = jnp.right_shift(iota(wide, 0), 4) == jnp.right_shift(iota(wide, 1), 4)
    earlier = jnp.logical_and(same, iota(wide, 1) < iota(wide, 0))
    order = jnp.sum(ones(jnp.logical_and(earlier, g_row == g_col)), axis=1, keepdims=True)
    lane = iota((1, 128), 1)
    part, label = jnp.right_shift(lane, 3), lane & 7
    own = sum(jnp.where(part == i, beta[i], 0) for i in range(PER))
    wanted = (label ^ own) ^ g_col
    seen = sum(ones(jnp.logical_and(part > i, wanted == beta[i])) for i in range(PER - 1))
    count = dot(ones(same).astype(BF), ones(g_col == label).astype(BF))
    square = (128, 128)
    by_part = ones(jnp.right_shift(iota(square, 0), 3) == iota(square, 1)).astype(BF)
    place = dot((seen * count).astype(BF), by_part) + order
    rows = iota((256, 1), 0)
    place = place.astype(I32) + (jnp.right_shift(rows, 4) & 3) * CAP_IN

    four = 4 * CAP_IN
    sym = [a_row ^ beta[i] for i in range(PER)]
    for k in range(4):
        at = slice(k * 64, (k + 1) * 64)
        for i in range(PER):
            hot[i * 64 : (i + 1) * 64, :] = ones(iota((64, four), 1) == place[at, i : i + 1]).astype(BF)
        for n, w in ((0, 256), (256, 256), (512, 128)):
            got = dot(hot[...], y_ref[k * four : (k + 1) * four, n : n + w])
            for i in range(PER):
                keep = sym[i][:, n : n + w] == g_col[at, :]
                eri[i * 256 + k * 64 : i * 256 + (k + 1) * 64, n : n + w] = jnp.where(
                    keep, got[i * 64 : (i + 1) * 64, :], 0.0
                ).astype(BF)

    _, slot_col, p_col = slots(pair_ref)
    from_slot = ones(iota((128, CAP_IN), 1) == slot_col).astype(BF)
    allowed = jnp.where(p_col == g_row, dot(from_slot, notes[0:CAP_IN, :].astype(BF)), 0.0).astype(BF)
    p_row = pair_ref[...]
    same2 = jnp.right_shift(iota(square, 0), 3) == jnp.right_shift(iota(square, 1), 3)
    earlier2 = jnp.logical_and(same2, iota(square, 0) < iota(square, 1))
    order2 = jnp.sum(ones(jnp.logical_and(earlier2, p_row == p_col)), axis=0, keepdims=True)
    row = iota((128, 1), 0)
    part2, label2 = jnp.right_shift(row, 3), row & 7
    own2 = sum(jnp.where(part2 == i, beta[i], 0) for i in range(PER))
    wanted2 = (label2 ^ own2) ^ p_row
    seen2 = sum(ones(jnp.logical_and(part2 > i, wanted2 == beta[i])) for i in range(PER - 1))
    count2 = dot(ones(label2 == p_row).astype(BF), ones(same2).astype(BF))
    short = (16, 128)
    by_part2 = ones(jnp.right_shift(iota(short, 1), 3) == iota(short, 0)).astype(BF)
    place2 = dot(by_part2, (seen2 * count2).astype(BF)) + order2
    place2 = place2.astype(I32) + jnp.right_shift(iota((1, 128), 1), 3) * CAP_OUT
    out_rows = LAYERS * CAP_OUT
    for i in range(PER):
        hot2[...] = ones(iota((out_rows, 128), 0) == place2[i : i + 1, :]).astype(BF)
        amp[:, i * 256 : (i + 1) * 256] = dot(hot2[...], allowed).astype(BF)
    for n, w in ((0, 256), (256, 256), (512, 128)):
        got = dot(amp[...], eri[:, n : n + w])
        x_ref[:, n : n + w] = got
        high = got.astype(BF).astype(F32)
        low = got - high
        for k in range(LAYERS):
            at = slice(k * CAP_OUT, k * CAP_OUT + CAP_LOW)
            stage[k * CAP_IN : k * CAP_IN + CAP_LOW, 0:w] = high[at, :]
            stage[k * CAP_IN + CAP_LOW : (k + 1) * CAP_IN, 0:w] = low[at, :]
        pair_out[:, n : n + w] = stage[:, 0:w].astype(BF)


def unpack_tables(stride, gap, pair, v_ref, hot, sym, j_ref):
    me = lax.axis_index("depth")
    labels = [pair[me * OWN_IJ + j] for j in range(OWN_IJ)]
    width = hot.shape[1]
    a_row, b_row = irreps(v_ref)
    count, order = class_counts(labels)
    for y in range(8):
        j_ref[y] = count[y]
    rank_row, rank_col, b_col = ranks(b_row)
    same = jnp.logical_and((rank_row & 15) == (rank_col & 15), rank_row < rank_col)
    diff = b_col ^ b_row
    before = [jnp.sum(ones(jnp.logical_and(same, diff == y)), axis=1, keepdims=True) for y in range(8)]
    first = (rank_col & 15) * stride
    for j in range(OWN_IJ):
        place = sum(j_ref[y ^ labels[j]].astype(F32) * before[y] for y in range(8)) + order[j].astype(F32)
        place = first + place.astype(I32)
        for t in range(2):
            mine = place[t * HALF : (t + 1) * HALF, :]
            lane = iota((HALF, width), 1)
            at = (t * OWN_IJ + j) * HALF
            hot[at : at + HALF, :] = ones(jnp.logical_or(lane == mine, lane == mine + gap)).astype(BF)
    sym[...] = b_col ^ a_row


def unpack_step(pair, hot, sym, terms, o_ref):
    step = pl.program_id(0)
    me = lax.axis_index("depth")
    rows = OWN_IJ * HALF
    of_step = hot[pl.ds(pl.multiple_of(step * rows, rows), rows), :]
    ab = sym[pl.ds(pl.multiple_of(step * HALF, HALF), HALF), :]
    for n, w, real in ((0, 256, 256), (256, 256, 256), (512, 128, A_ROWS - 512)):
        got = dot(of_step, terms[:, n : n + w])
        for j in range(OWN_IJ):
            label = pair[me * OWN_IJ + j]
            part = jnp.where(ab[:, n : n + w] == label, got[j * HALF : (j + 1) * HALF, :], 0.0)
            o_ref[:, j * A_ROWS + n : j * A_ROWS + n + real] = part[:, :real]


def unpack_kernel(pair, hot, sym, y_ref, o_ref):
    unpack_step(pair, hot, sym, y_ref, o_ref)


def full_unpack_kernel(pair, v_ref, y_ref, o_ref, hot, both, sym, j_ref):
    @pl.when(pl.program_id(0) == 0)
    def _():
        gap = LAYERS * CAP_OUT
        unpack_tables(CAP_OUT, gap, pair, v_ref, hot, sym, j_ref)
        whole = y_ref[...]
        top = whole.astype(BF)
        both[0:gap, :] = top
        both[gap : 2 * gap, :] = (whole - top.astype(F32)).astype(BF)

    unpack_step(pair, hot, sym, both, o_ref)


def table_kernel(pair, v_ref, hot, sym, j_ref):
    unpack_tables(CAP_IN, CAP_LOW, pair, v_ref, hot, sym, j_ref)


VM = pl.BlockSpec(memory_space=pltpu.VMEM)
SM = pl.BlockSpec(memory_space=pltpu.SMEM)


def call(kernel, args, specs, out, scratch, flops, moved, outs=VM):
    return pl.pallas_call(
        kernel,
        out_shape=out,
        in_specs=specs,
        out_specs=outs,
        scratch_shapes=scratch,
        compiler_params=pltpu.CompilerParams(vmem_limit_bytes=VMEM_LIMIT),
        cost_estimate=pl.CostEstimate(flops=flops, bytes_accessed=moved, transcendentals=0),
    )(*args)


def dense(rows, held, integrals, virt_irrep, pair_irrep):
    rows = rows.reshape(LAYERS, OWN_IJ, CDS)
    at = jnp.arange(LAYERS)
    apart = lax.axis_index("col") ^ (at & 7)
    at = (lax.axis_index("row") ^ (at >> 3)) + 2 * (apart >> 2) + 4 * (apart & 1) + 8 * (apart >> 1 & 1)
    amps = jnp.take(rows, at, axis=0).reshape(1, LAYERS * OWN_IJ, CDS)
    amps = jnp.broadcast_to(amps, (LAYERS, LAYERS * OWN_IJ, CDS))
    amps = lax.all_to_all(amps, "depth", 0, 0, tiled=True).transpose(1, 0, 2).reshape(-1, LAYERS * CDS)
    pair_sym = held[:, 0, A_ROWS + CDS : A_ROWS + 2 * CDS].reshape(-1).astype(I32)
    allowed = jnp.where(pair_irrep[:, None] == pair_sym[None, :], amps, jnp.zeros_like(amps))
    share = B_PAD // LAYERS
    padded = jnp.pad(integrals, ((0, B_PAD - B_COLS), (0, 0))).reshape(LAYERS, share, CDS * A_ROWS)
    piece = lax.all_to_all(padded, "depth", 0, 0, tiled=True).reshape(LAYERS, share, CDS, A_ROWS)
    full = jnp.einsum("jsc,sbca->jba", allowed.reshape(-1, LAYERS, CDS), piece, preferred_element_type=F32)
    back = lax.all_to_all(full, "depth", 0, 0, tiled=True).reshape(LAYERS, OWN_IJ, share, A_ROWS)
    mine = back.transpose(0, 2, 1, 3).reshape(B_PAD, OWN_IJ, A_ROWS)[:B_COLS]
    irrep_a = lax.dynamic_slice_in_dim(virt_irrep, lax.axis_index("row") * A_ROWS, A_ROWS, 0)
    irrep_b = lax.dynamic_slice_in_dim(virt_irrep, lax.axis_index("col") * B_COLS, B_COLS, 0)
    irrep_ij = lax.dynamic_slice_in_dim(pair_irrep, lax.axis_index("depth") * OWN_IJ, OWN_IJ, 0)
    ab_sym = jnp.bitwise_xor(irrep_b[:, None], irrep_a[None, :])
    mask = irrep_ij[None, :, None] == ab_sym[:, None, :]
    return jnp.where(mask, mine, jnp.float32(0.0)).reshape(B_COLS, OWN_IJ * A_ROWS)


def swap(array, axis, size, step):
    return lax.ppermute(array, axis, [(d, d ^ step) for d in range(size)])


def body(amplitudes, integrals, virt_irrep, pair_irrep, panel_c, panel_d):
    rows = LAYERS * CAP_IN
    out_rows = LAYERS * CAP_OUT
    p_row = pair_irrep[None, :]
    v_row = jnp.concatenate([virt_irrep, panel_c, panel_d, jnp.zeros(TURN - NV - 2 * CDS, I32)])[None, :]
    amps = jnp.concatenate([amplitudes, swap(amplitudes, "row", 2, 1)], axis=0)
    amps, v_row = lax.optimization_barrier((amps, v_row))
    far = swap(amps, "col", 8, 4)
    place, notes = call(
        place_kernel,
        (v_row, pair_irrep, v_row, p_row),
        [SM, SM, VM, VM],
        (jax.ShapeDtypeStruct((8, CDS * B_PAD), I32), jax.ShapeDtypeStruct((CAP_IN, 128), F32)),
        [pltpu.VMEM((8, B_PAD), F32), pltpu.VMEM((8, 256), I32)],
        2 * 10**10,
        10**5,
        (VM, VM),
    )
    far, place, notes = lax.optimization_barrier((far, place, notes))
    amps = jnp.concatenate([amps, far], axis=0)
    amps, v_row = lax.optimization_barrier((amps, v_row))
    near = swap(amps, "col", 8, 1)
    hot, sym = call(
        table_kernel,
        (pair_irrep, v_row),
        [SM, VM],
        (
            jax.ShapeDtypeStruct((2 * OWN_IJ * HALF, rows), BF),
            jax.ShapeDtypeStruct((B_PAD, A_PAD), I32),
        ),
        [pltpu.SMEM((8,), I32)],
        10**9,
        10**6,
        (VM, VM),
    )
    near, hot, sym, place = lax.optimization_barrier((near, hot, sym, place))
    amps = jnp.concatenate([amps, near], axis=0)
    amps = jnp.concatenate([amps, swap(amps, "col", 8, 2)], axis=0)
    sent = call(
        pack_kernel,
        (notes, v_row, place, integrals),
        [VM] * 4,
        jax.ShapeDtypeStruct((rows, A_PAD), BF),
        [
            pltpu.VMEM((rows, CDS * B_PAD), BF),
            pltpu.VMEM((CDS * B_PAD, A_PAD), BF),
        ],
        2 * rows * CDS * B_PAD * A_PAD,
        2 * B_COLS * CDS * A_ROWS,
    )
    last = pl.BlockSpec((rows, 128), lambda n: (0, A_PAD // 128 - 1))
    sent = pl.pallas_call(
        note_kernel,
        out_shape=jax.ShapeDtypeStruct((rows, A_PAD), BF),
        grid=(1,),
        in_specs=[
            pl.BlockSpec((CAP_IN, 128), lambda n: (0, 0)),
            pl.BlockSpec((1, 128), lambda n: (0, 0)),
            pl.BlockSpec((128, CDS), lambda n: (0, 0)),
            last,
        ],
        out_specs=last,
        scratch_shapes=[pltpu.VMEM((CAP_IN, 128), F32), pltpu.VMEM((128, CDS), F32)],
        input_output_aliases={3: 0},
        compiler_params=pltpu.CompilerParams(vmem_limit_bytes=VMEM_LIMIT),
        cost_estimate=pl.CostEstimate(flops=10**7, bytes_accessed=4 * rows * 128, transcendentals=0),
    )(notes, p_row, amps, sent)
    held = lax.all_to_all(sent.reshape(LAYERS, CAP_IN, A_PAD), "depth", 0, 0, tiled=True)
    part, terms, over = call(
        compute_kernel,
        (v_row, p_row, held.reshape(rows, A_PAD)),
        [VM] * 3,
        (
            jax.ShapeDtypeStruct((out_rows, A_PAD), F32),
            jax.ShapeDtypeStruct((rows, A_PAD), BF),
            jax.ShapeDtypeStruct((1,), I32),
        ),
        [
            pltpu.VMEM((PER * 64, 4 * CAP_IN), BF),
            pltpu.VMEM((PER * 256, A_PAD), BF),
            pltpu.VMEM((out_rows, PER * 256), BF),
            pltpu.VMEM((out_rows, 128), BF),
            pltpu.VMEM((CAP_IN + 8, LAYERS * CDS), F32),
            pltpu.VMEM((rows, 128), F32),
            pltpu.VMEM((rows, 256), F32),
        ],
        2 * PER * 256 * A_PAD * (out_rows + 4 * CAP_IN),
        2 * rows * A_PAD,
        (VM, VM, SM),
    )


    def finish(kernel, array, extra, specs, scratch):
        chunks = array.reshape(LAYERS, -1, A_PAD)
        back = lax.all_to_all(chunks, "depth", 0, 0, tiled=True)
        return pl.pallas_call(
            kernel,
            out_shape=jax.ShapeDtypeStruct((B_COLS, OWN_IJ * A_ROWS), F32),
            grid=(2,),
            in_specs=[SM, *specs, whole(array.shape)],
            out_specs=pl.BlockSpec((HALF, OWN_IJ * A_ROWS), lambda t: (t, 0)),
            scratch_shapes=scratch,
            compiler_params=pltpu.CompilerParams(vmem_limit_bytes=VMEM_LIMIT),
            cost_estimate=pl.CostEstimate(
                flops=4 * OWN_IJ * HALF * rows * A_PAD,
                bytes_accessed=4 * B_COLS * OWN_IJ * A_ROWS,
                transcendentals=0,
            ),
        )(pair_irrep, *extra, back.reshape(array.shape))

    def whole(shape):
        return pl.BlockSpec(shape, lambda t: (0, 0))

    def usual(part, terms, held, amps, hot, sym):
        return finish(unpack_kernel, terms, (hot, sym), [whole(hot.shape), whole(sym.shape)], [])

    def fuller(part, terms, held, amps, hot, sym):
        scratch = [
            pltpu.VMEM((2 * OWN_IJ * HALF, 2 * out_rows), BF),
            pltpu.VMEM((2 * out_rows, A_PAD), BF),
            pltpu.VMEM((B_PAD, A_PAD), I32),
            pltpu.SMEM((8,), I32),
        ]
        return finish(full_unpack_kernel, part, (v_row,), [whole((1, TURN))], scratch)

    def general(part, terms, held, amps, hot, sym):
        return dense(amps, held, integrals, virt_irrep, pair_irrep)

    return lax.switch(over[0], (usual, fuller, general), part, terms, held, amps, hot, sym)


def solution(mesh):
    return jax.shard_map(
        body,
        mesh=mesh,
        in_specs=(
            P(("row", "col"), "depth"),
            P("col", ("row", "depth")),
            P(),
            P(),
            P("depth"),
            P("depth"),
        ),
        out_specs=P("col", ("row", "depth")),
        check_vma=False,
    )
```
